32 devices in a mesh: grp: 2 (over y), own: 4 (over z), hlp: 4 (over x, core).
Axes of the slice: x: 2, y: 2, z: 4, core: 2. Of those that a mesh axis runs over, the one named last changes fastest.
Arguments:
- points: bfloat16 [8192, 1024], P(('grp', 'own', 'hlp')), parts along dimension 0, may hold values from -24 to 24
- cluster_of: int32 [8192], P(('grp', 'own', 'hlp')), parts along dimension 0, may hold values from 0 to 3, as said below
- subcentroids: bfloat16 [8, 256, 1024], P(('grp', 'own'), 'hlp'), parts along dimension 0, may hold values from -3 to 3
Outputs:
- refined: float32 [8, 256, 1024], P(('grp', 'own'), 'hlp'), parts along dimension 0
- log_resp: float32 [8192, 256], P(('grp', 'own', 'hlp')), parts along dimension 0
The draws below stay inside these ranges and needn't reach their ends.
There are 2 independent parts, one for each index of `grp`. The reference program is written for one: setup_inputs(seed, part) draws one part's arguments, and reference() takes and returns one part's arrays. A program takes and returns all parts, laid end to end along the dimension named above; each array names one. Nothing has to cross between parts.
Inputs may be any that keep to these rules, and one draw needn't show every extreme that they name: `cluster_of`: the points of one device name each cluster at most 128 times; in every draw one cluster is named exactly 128 times by the points of every device.
All inputs are finite; a program needn't handle non-finite values.
Results may differ from the reference program's by a relative error of at most 0.0097.
Values may be sent and summed in bfloat16 or wider, within the bound.
No kernel may reach another device: no remote copies, remote signals or barrier semaphores. Data moves between devices by JAX's collectives and lax.ppermute only.
A program may use at most 64 MiB of HBM per device.

```python
import jax
import jax.numpy as jnp
from jax import lax

D = 1024
K = 256
ITERS = 2
ROWS_DEV = 256
CLUSTERS = 4
CAP = 128
ROWS = 4096


def cluster_plan(key):
    key = jax.random.fold_in(key, 11)
    first_key, run_key, start_key, order_key = jax.random.split(key, 4)
    devices = ROWS // ROWS_DEV
    favourite = jax.random.randint(first_key, (), 0, CLUSTERS)
    remainder = ROWS_DEV - CAP
    least = max((remainder + CLUSTERS - 2) // (CLUSTERS - 1), 1)
    lengths = jax.random.randint(run_key, (devices, 1), least, CAP + 1)
    begins = jax.random.randint(start_key, (devices, 1), 0, CLUSTERS - 1)
    counter = jnp.arange(remainder, dtype=jnp.int32)[None, :]
    others = (favourite + 1 + (begins + counter // lengths) % (CLUSTERS - 1)) % CLUSTERS
    labels = jnp.concatenate([jnp.full((devices, CAP), favourite, jnp.int32), others.astype(jnp.int32)], axis=1)
    noise = jax.random.randint(order_key, (devices, ROWS_DEV), 0, 1 << 18) * ROWS_DEV + jnp.arange(ROWS_DEV, dtype=jnp.int32)[None, :]
    order = jnp.argsort(noise, axis=1)
    return jnp.take_along_axis(labels, order, axis=1).reshape(-1).astype(jnp.int32)


def centroid_table(key):
    key = jax.random.fold_in(key, 5)
    return jnp.clip(0.5 * jax.random.normal(key, (CLUSTERS, K, D), jnp.float32), -3.0, 3.0)


def draw_cluster_of(key, part):
    return cluster_plan(key)


def draw_subcentroids(key, part):
    return centroid_table(key).astype(jnp.bfloat16)


def draw_points(key, part):
    fresh = jax.random.fold_in(key, 23)
    return jnp.clip(jax.random.normal(fresh, (ROWS, D), jnp.float32), -6.0, 6.0).astype(jnp.bfloat16)


def setup_inputs(seed: int = 0, part: int = 0) -> dict:
    key_of = jax.random.split(jax.random.key(seed), 4)
    part_keys = jax.random.split(jax.random.fold_in(key_of[3], part), 4)
    return {
        "points": draw_points(jax.random.fold_in(jax.random.fold_in(key_of[3], part), 71), part),
        "cluster_of": draw_cluster_of(jax.random.fold_in(jax.random.fold_in(key_of[3], part), 71), part),
        "subcentroids": draw_subcentroids(jax.random.fold_in(jax.random.fold_in(key_of[3], part), 71), part),
    }


smoothing_factor = 16.0
prior_count = 1.0
span = 512


def closeness_matrix(vector_samples, group_prototypes):
    return lax.dot_general(vector_samples, group_prototypes, (((1,), (1,)), ((), ())), preferred_element_type=jnp.float32)


def weight_logarithms(vector_samples, group_prototypes, elementwise_power):
    membership_energies = (2.0 * closeness_matrix(vector_samples, group_prototypes) - elementwise_power[None, :]) / smoothing_factor
    top = jnp.max(membership_energies, axis=1, keepdims=True)
    total = jnp.log(jnp.sum(jnp.exp(membership_energies - top), axis=1, keepdims=True))
    return membership_energies - (top + total)


def reference(points, cluster_of, subcentroids):
    total = points.shape[0]
    labels = jnp.arange(CLUSTERS, dtype=jnp.int32)
    member_tallies = jnp.sum((cluster_of[:, None] == labels[None, :]).astype(jnp.int32), axis=0)
    order = jnp.argsort(cluster_of, stable=True).astype(jnp.int32)
    starts = jnp.cumsum(member_tallies) - member_tallies
    pieces = (member_tallies + span - 1) // span
    ends = jnp.cumsum(pieces)
    first = ends - pieces
    blocks = total // span + CLUSTERS
    number = jnp.arange(blocks, dtype=jnp.int32)
    owner = jnp.minimum(jnp.sum((ends[None, :] <= number[:, None]).astype(jnp.int32), axis=1), CLUSTERS - 1)
    local = number - first[owner]
    offset = local[:, None] * span + jnp.arange(span, dtype=jnp.int32)[None, :]
    valid = (offset < member_tallies[owner][:, None]) & (number < ends[-1])[:, None]
    picked = order[jnp.clip(starts[owner][:, None] + offset, 0, total - 1)]
    group_prototypes = subcentroids
    refined = subcentroids.astype(jnp.float32)
    for turn in range(ITERS):
        elementwise_power = jnp.sum(jnp.square(group_prototypes.astype(jnp.float32)), axis=2)

        def advance(carry, item):
            sums, mass = carry
            cluster, picks, live = item
            vector_samples = points[picks]
            share = jnp.exp(weight_logarithms(vector_samples, group_prototypes[cluster], elementwise_power[cluster]))
            share = jnp.where(live[:, None], share, 0.0).astype(jnp.bfloat16)
            part = lax.dot_general(share, vector_samples, (((0,), (0,)), ((), ())), preferred_element_type=jnp.float32)
            sums = sums.at[cluster].add(part)
            mass = mass.at[cluster].add(jnp.sum(share.astype(jnp.float32), axis=0))
            return (sums, mass), None

        initial_sums = jnp.zeros((CLUSTERS, K, D), jnp.float32)
        start_mass = jnp.zeros((CLUSTERS, K), jnp.float32)
        (sums, mass), unused = lax.scan(advance, (initial_sums, start_mass), (owner, picked, valid))
        refined = (sums + prior_count * group_prototypes.astype(jnp.float32)) / (mass[:, :, None] + prior_count)
        group_prototypes = refined.astype(jnp.bfloat16)
    elementwise_power = jnp.sum(jnp.square(group_prototypes.astype(jnp.float32)), axis=2)

    def finish(item):
        cluster, picks, live = item
        return weight_logarithms(points[picks], group_prototypes[cluster], elementwise_power[cluster])

    logs = lax.map(finish, (owner, picked, valid))
    target = jnp.where(valid, picked, total).reshape(-1)
    log_resp = jnp.zeros((total, K), jnp.float32).at[target].set(logs.reshape(-1, K), mode="drop")
    return refined, log_resp
```

```python
import functools

import jax
import jax.numpy as jnp
from jax import lax
from jax.experimental import pallas as pl
from jax.experimental.pallas import tpu as pltpu
from jax.sharding import PartitionSpec as P

ITERS = 2
GROUPS = 4
TILE = 256

smoothing_factor = 16.0
prior_count = 1.0

EMPTY = 64.0
LIMIT = 32.0

BF = jnp.bfloat16
F32 = jnp.float32
NT = (((1,), (1,)), ((), ()))
NN = (((1,), (0,)), ((), ()))


def matmul(a, b, dims):
    return lax.dot_general(a, b, dims, preferred_element_type=F32)


def slots_of(me, cluster, depth, owners):
    count = cluster.shape[1]
    height = max(16, owners)
    offset = jnp.bitwise_xor(cluster, me)
    member = lax.broadcasted_iota(jnp.int32, (height, count), 0) == offset
    earlier = lax.broadcasted_iota(jnp.int32, (count, count), 0) < lax.broadcasted_iota(
        jnp.int32, (count, count), 1
    )
    member = jnp.where(member, 1.0, 0.0)
    before = matmul(member.astype(BF), jnp.where(earlier, 1.0, 0.0).astype(BF), NN)
    rank = jnp.sum(before * member, axis=0, keepdims=True).astype(jnp.int32)
    return offset * depth + rank, jnp.sum(member, axis=1, keepdims=True)


def pack_kernel(depth, owners, me_ref, cluster_ref, points_ref, *outs):
    slot, tally = slots_of(me_ref[0], cluster_ref[...], depth, owners)
    points = points_ref[...]
    height = outs[0].shape[0]
    per = height // depth
    for g, out in enumerate(outs):
        rows = lax.broadcasted_iota(jnp.int32, (height, points.shape[0]), 0) + g * height
        pick = jnp.where(rows == slot, 1.0, 0.0).astype(BF)
        block = matmul(pick, points, NN)
        for j in range(per):
            held = tally[g * per + j : g * per + j + 1, :].astype(jnp.int32)
            local = lax.broadcasted_iota(jnp.int32, (depth, 1), 0)
            part = block[j * depth : (j + 1) * depth]
            out[j * depth : (j + 1) * depth, :] = jnp.where(local < held, part, EMPTY).astype(BF)


def unpack_kernel(depth, owners, me_ref, cluster_ref, *refs):
    *logs, out = refs
    slot, _ = slots_of(me_ref[0], cluster_ref[...], depth, owners)
    count = slot.shape[1]
    column = jnp.broadcast_to(slot.astype(F32), (128, count)).T[:, 0:1].astype(jnp.int32)
    width = logs[0].shape[1]
    total = None
    for g, block in enumerate(logs):
        lanes = lax.broadcasted_iota(jnp.int32, (count, width), 1) + g * width
        pick = jnp.where(lanes == column, 1.0, 0.0).astype(BF)
        term = matmul(pick, block[...], NT)
        total = term if total is None else total + term
    out[...] = total


def square_norms(centres):
    wide = centres.astype(F32)
    return jnp.sum(wide * wide, axis=1, keepdims=True)


def tiles_of(refs):
    tiles, held, size = [], [], 0
    for ref in refs:
        rows = ref.shape[0]
        if rows >= TILE:
            for start in range(0, rows, TILE):
                tiles.append([ref[start : start + TILE, :]])
            continue
        held.append(ref[...])
        size += rows
        if size == TILE:
            tiles.append(held)
            held, size = [], 0
    if held:
        tiles.append(held)
    return [parts[0] if len(parts) == 1 else jnp.concatenate(parts, axis=0) for parts in tiles]


def energies(centres, norms, rows):
    return matmul(centres, rows, NT) * (2.0 / smoothing_factor) - norms * (1.0 / smoothing_factor)


def live_columns(rows):
    first = lax.broadcasted_iota(jnp.int32, (16, 128), 1) == 0
    value = matmul(jnp.where(first, 1.0, 0.0).astype(BF), rows[:, :128], NT)[0:1]
    return jnp.where(value < LIMIT, 1.0, 0.0)


def accumulate(centres, norms, rows, sums_ref, mass_ref, fresh):
    logits = energies(centres, norms, rows)
    top = jnp.max(logits, axis=0, keepdims=True)
    weight = jnp.exp(logits - top)
    scale = live_columns(rows) / jnp.sum(weight, axis=0, keepdims=True)
    share = (weight * scale).astype(BF)
    wide = share.astype(F32)
    mass = wide[:, 0:128]
    for start in range(128, wide.shape[1], 128):
        mass = mass + wide[:, start : start + 128]
    part = matmul(share, rows, NN)
    if fresh:
        mass_ref[...] = mass
        sums_ref[...] = part
    else:
        mass_ref[...] += mass
        sums_ref[...] += part


def first_kernel(centres_ref, *refs):
    *rows, sums_ref, mass_ref = refs
    centres = centres_ref[...]
    norms = square_norms(centres)
    for i, tile in enumerate(tiles_of(rows)):
        accumulate(centres, norms, tile, sums_ref, mass_ref, i == 0)


def next_kernel(centres_ref, old_sums, old_mass, *refs):
    *rows, sums_ref, mass_ref = refs
    centres = centres_ref[...]
    norms = square_norms(centres)
    sums_ref[...] = old_sums[...]
    mass_ref[...] = old_mass[...]
    for tile in tiles_of(rows):
        accumulate(centres, norms, tile, sums_ref, mass_ref, False)


def refine(centres, sums_ref, mass_ref):
    mass = jnp.sum(mass_ref[...], axis=1, keepdims=True)
    return (sums_ref[...] + prior_count * centres.astype(F32)) / (mass + prior_count)


def last_kernel(counts, share_rows, helper_ref, centres_ref, old_sums, old_mass, *refs):
    earlier, late, own = counts
    rows = refs[: earlier + late]
    refined_ref, *logs = refs[earlier + late : earlier + late + 1 + own]
    sums_ref, mass_ref = refs[earlier + late + 1 + own :]
    helper = helper_ref[0]
    centres = centres_ref[...]
    norms = square_norms(centres)
    sums_ref[...] = old_sums[...]
    mass_ref[...] = old_mass[...]
    for tile in tiles_of(rows[earlier:]):
        accumulate(centres, norms, tile, sums_ref, mass_ref, False)
    for turn in range(1, ITERS):
        centres = refine(centres, sums_ref, mass_ref).astype(BF)
        norms = square_norms(centres)
        for i, tile in enumerate(tiles_of(rows)):
            accumulate(centres, norms, tile, sums_ref, mass_ref, i == 0)
    refined = refine(centres, sums_ref, mass_ref)
    refined_ref[...] = refined[0:share_rows]
    centres = refined.astype(BF)
    norms = square_norms(centres)
    parts = (earlier + late) // own
    for g, out in enumerate(logs):
        logits = energies(centres, norms, rows[g * parts][...])
        top = jnp.max(logits, axis=0, keepdims=True)
        total = jnp.log(jnp.sum(jnp.exp(logits - top), axis=0, keepdims=True))
        result = (logits - (top + total)).astype(BF)
        for j in range(centres.shape[0] // share_rows):
            place = pl.multiple_of(jnp.bitwise_xor(helper, j) * share_rows, share_rows)
            out[pl.ds(place, share_rows), :] = result[j * share_rows : (j + 1) * share_rows]


def vmem(n):
    return [pl.BlockSpec(memory_space=pltpu.VMEM)] * n


SMEM = pl.BlockSpec(memory_space=pltpu.SMEM)
PARAMS = pltpu.CompilerParams(vmem_limit_bytes=56 * 1024 * 1024)


def hop(axis, size, step):
    pairs = [(i, i ^ step) for i in range(size)]
    return lambda x: lax.ppermute(x, axis, pairs)


def per_device(points, cluster_of, subcentroids):
    count, width = points.shape
    owners = lax.axis_size("own")
    helpers = lax.axis_size("hlp")
    depth = min(count // 2, 4 * count // owners)
    share_rows = subcentroids.shape[1]
    subs = share_rows * helpers
    groups = min(GROUPS, owners)
    per = owners // groups
    height = per * depth

    me = lax.axis_index("own").astype(jnp.int32).reshape(1)
    helper = lax.axis_index("hlp").astype(jnp.int32).reshape(1)
    cluster = cluster_of.reshape(1, count)

    packed = pl.pallas_call(
        functools.partial(pack_kernel, depth, owners),
        out_shape=[jax.ShapeDtypeStruct((height, width), BF)] * groups,
        in_specs=[SMEM] + vmem(2),
        out_specs=vmem(groups),
        compiler_params=PARAMS,
        name="pack",
    )(me, cluster, points)

    def across(blocks, g, axis):
        done = []
        for j in range(per):
            step = g * per + j
            piece = blocks if per == 1 else lax.slice_in_dim(blocks, j * depth, (j + 1) * depth, axis=axis)
            done.append(piece if step == 0 else hop("own", owners, step)(piece))
        return done[0] if per == 1 else jnp.concatenate(done, axis=axis)

    def spread(block):
        held = {0: block}
        for step in range(2, helpers, 2):
            held[step] = hop("hlp", helpers, step)(block)
        for step in range(0, helpers, 2):
            held[step + 1] = hop("hlp", helpers, 1)(held[step])
        return [held[j] for j in range(helpers)]

    start = jnp.concatenate(spread(subcentroids[0]), axis=0)
    rows = [spread(across(packed[g], g, 0)) for g in range(groups)]

    state = [jax.ShapeDtypeStruct((subs, width), F32), jax.ShapeDtypeStruct((subs, 128), F32)]
    sums, mass = pl.pallas_call(
        first_kernel,
        out_shape=state,
        in_specs=vmem(1 + helpers),
        out_specs=vmem(2),
        compiler_params=PARAMS,
        name="first_rows",
    )(start, *rows[0])
    for g in range(1, groups - 1):
        sums, mass = pl.pallas_call(
            next_kernel,
            out_shape=state,
            in_specs=vmem(3 + helpers),
            out_specs=vmem(2),
            compiler_params=PARAMS,
            name="more_rows",
        )(start, sums, mass, *rows[g])
    earlier = [r for part in rows[: groups - 1] for r in part]
    late = rows[groups - 1]
    refined, *logs = pl.pallas_call(
        functools.partial(last_kernel, (len(earlier), len(late), groups), share_rows),
        out_shape=[jax.ShapeDtypeStruct((share_rows, width), F32)]
        + [jax.ShapeDtypeStruct((subs, height), BF)] * groups,
        in_specs=[SMEM] + vmem(3 + len(earlier) + len(late)),
        out_specs=vmem(1 + groups),
        scratch_shapes=[pltpu.VMEM((subs, width), F32), pltpu.VMEM((subs, 128), F32)],
        compiler_params=PARAMS,
        name="rounds",
    )(helper, start, sums, mass, *earlier, *late)

    back = [across(logs[g], g, 1) for g in range(groups)]
    log_resp = pl.pallas_call(
        functools.partial(unpack_kernel, depth, owners),
        out_shape=jax.ShapeDtypeStruct((count, subs), F32),
        in_specs=[SMEM] + vmem(1 + groups),
        out_specs=pl.BlockSpec(memory_space=pltpu.VMEM),
        compiler_params=PARAMS,
        name="unpack",
    )(me, cluster, *back)
    return (refined[None], log_resp)


def solution(mesh):
    in_specs = (
        P(("grp", "own", "hlp"), None),
        P(("grp", "own", "hlp")),
        P(("grp", "own"), "hlp", None),
    )
    out_specs = (P(("grp", "own"), "hlp", None), P(("grp", "own", "hlp"), None))
    return jax.shard_map(
        per_device, mesh=mesh, in_specs=in_specs, out_specs=out_specs, check_vma=False
    )
```

```python
import functools
import math

import jax
import jax.numpy as jnp
from jax import lax
from jax.experimental import pallas as pl
from jax.experimental.pallas import tpu as pltpu
from jax.sharding import PartitionSpec as P

ITERS = 2
GROUPS = 4
TILE = 256

smoothing_factor = 16.0
prior_count = 1.0

EMPTY = 64.0
LIMIT = 32.0

BF = jnp.bfloat16
F32 = jnp.float32
TN = (((0,), (0,)), ((), ()))
NN = (((1,), (0,)), ((), ()))


def matmul(a, b, dims):
    return lax.dot_general(a, b, dims, preferred_element_type=F32)


def slots_of(me, cluster, depth, owners):
    count = cluster.shape[1]
    height = max(16, owners)
    offset = jnp.bitwise_xor(cluster, me)
    member = lax.broadcasted_iota(jnp.int32, (height, count), 0) == offset
    earlier = lax.broadcasted_iota(jnp.int32, (count, count), 0) < lax.broadcasted_iota(
        jnp.int32, (count, count), 1
    )
    member = jnp.where(member, 1.0, 0.0)
    before = matmul(member.astype(BF), jnp.where(earlier, 1.0, 0.0).astype(BF), NN)
    rank = jnp.sum(before * member, axis=0, keepdims=True).astype(jnp.int32)
    return offset * depth + rank, jnp.sum(member, axis=1, keepdims=True)


def pack_kernel(depth, owners, me_ref, cluster_ref, points_ref, *outs):
    slot, tally = slots_of(me_ref[0], cluster_ref[...], depth, owners)
    points = points_ref[...]
    height = outs[0].shape[0]
    per = height // depth
    for g, out in enumerate(outs):
        rows = lax.broadcasted_iota(jnp.int32, (height, points.shape[0]), 0) + g * height
        pick = jnp.where(rows == slot, 1.0, 0.0).astype(BF)
        block = matmul(pick, points, NN)
        for j in range(per):
            held = tally[g * per + j : g * per + j + 1, :].astype(jnp.int32)
            local = lax.broadcasted_iota(jnp.int32, (depth, 1), 0)
            part = block[j * depth : (j + 1) * depth]
            out[j * depth : (j + 1) * depth, :] = jnp.where(local < held, part, EMPTY).astype(BF)


def unpack_kernel(depth, owners, me_ref, cluster_ref, *refs):
    *logs, out = refs
    slot, _ = slots_of(me_ref[0], cluster_ref[...], depth, owners)
    count = slot.shape[1]
    column = jnp.broadcast_to(slot.astype(F32), (128, count)).T[:, 0:1].astype(jnp.int32)
    height = logs[0].shape[0]
    total = None
    for g, block in enumerate(logs):
        lanes = lax.broadcasted_iota(jnp.int32, (count, height), 1) + g * height
        pick = jnp.where(lanes == column, 1.0, 0.0).astype(BF)
        term = matmul(pick, block[...], NN)
        total = term if total is None else total + term
    out[...] = total


def square_norms(centres):
    wide = centres.astype(F32)
    column = jnp.sum(wide * wide, axis=1, keepdims=True)
    return jnp.broadcast_to(column, (column.shape[0], 128)).T[0:1]


def tiles_of(refs):
    tiles, held, size = [], [], 0
    for ref in refs:
        rows = ref.shape[0]
        if rows >= TILE:
            for start in range(0, rows, TILE):
                tiles.append([ref[start : start + TILE, :]])
            continue
        held.append(ref[...])
        size += rows
        if size == TILE:
            tiles.append(held)
            held, size = [], 0
    if held:
        tiles.append(held)
    return [joined(parts) for parts in tiles]


def joined(parts):
    return parts[0] if len(parts) == 1 else jnp.concatenate(parts, axis=0)


def energies(turned, norms, rows):
    return matmul(rows, turned, NN) * (2.0 / smoothing_factor) - norms * (1.0 / smoothing_factor)


def accumulate(turned, norms, tiles, share_ref, sums_ref, mass_ref, fresh):
    start = 0
    for rows in tiles:
        logits = energies(turned, norms, rows)
        top = jnp.max(logits, axis=1, keepdims=True)
        weight = jnp.exp(logits - top)
        live = jnp.where(rows[:, 0:1].astype(F32) < LIMIT, 1.0, 0.0)
        scale = live / jnp.sum(weight, axis=1, keepdims=True)
        share_ref[start : start + rows.shape[0], :] = (weight * scale).astype(BF)
        start += rows.shape[0]
    start = 0
    for i, rows in enumerate(tiles):
        share = share_ref[start : start + rows.shape[0], :]
        mass = matmul(share, jnp.ones((rows.shape[0], 128), BF), TN)
        part = matmul(share, rows, TN)
        if fresh and i == 0:
            mass_ref[...] = mass
            sums_ref[...] = part
        else:
            mass_ref[...] += mass
            sums_ref[...] += part
        start += rows.shape[0]


def first_kernel(helpers, *refs):
    centres = joined([ref[...] for ref in refs[:helpers]])
    *rows, sums_ref, mass_ref, share_ref = refs[helpers:]
    accumulate(centres.T, square_norms(centres), tiles_of(rows), share_ref, sums_ref, mass_ref, True)


def refine(centres, sums_ref, mass_ref):
    mass = mass_ref[:, 0:1]
    return (sums_ref[...] + prior_count * centres.astype(F32)) / (mass + prior_count)


def last_kernel(helpers, counts, share_rows, helper_ref, *refs):
    earlier, late, own = counts
    centres = joined([ref[...] for ref in refs[:helpers]])
    old_sums, old_mass, *refs = refs[helpers:]
    given = refs[: earlier + late]
    refined_ref, *logs = refs[earlier + late : earlier + late + 1 + own]
    sums_ref, mass_ref, ordered, share_ref, rows, arrived = refs[earlier + late + 1 + own :]
    height = given[0].shape[0]
    copies = [
        pltpu.make_async_copy(ref, rows.at[i * height : (i + 1) * height], arrived.at[i])
        for i, ref in enumerate(given)
    ]
    for copy in copies[earlier:] + copies[:earlier]:
        copy.start()
    helper = helper_ref[0]
    norms = square_norms(centres)
    turned = centres.T
    sums_ref[...] = old_sums[...]
    mass_ref[...] = old_mass[...]
    for copy in copies[earlier:]:
        copy.wait()

    def tiles(first, last):
        return [rows[r : r + TILE, :] for r in range(first * height, last * height, TILE)]

    accumulate(turned, norms, tiles(earlier, earlier + late), share_ref, sums_ref, mass_ref, False)
    for copy in copies[:earlier]:
        copy.wait()
    for turn in range(1, ITERS):
        centres = refine(centres, sums_ref, mass_ref).astype(BF)
        norms = square_norms(centres)
        turned = centres.T
        accumulate(turned, norms, tiles(0, earlier + late), share_ref, sums_ref, mass_ref, True)
    refined = refine(centres, sums_ref, mass_ref)
    refined_ref[...] = refined[0:share_rows]
    centres = refined.astype(BF)
    for j in range(helpers):
        place = pl.multiple_of(jnp.bitwise_xor(helper, j) * share_rows, share_rows)
        ordered[pl.ds(place, share_rows), :] = centres[j * share_rows : (j + 1) * share_rows]
    centres = ordered[...]
    norms = square_norms(centres)
    turned = centres.T
    for g, out in enumerate(logs):
        first = g * helpers * height
        logits = energies(turned, norms, rows[first : first + height, :])
        top = jnp.max(logits, axis=1, keepdims=True)
        total = jnp.log(jnp.sum(jnp.exp(logits - top), axis=1, keepdims=True))
        out[...] = (logits - (top + total)).astype(BF)


def vmem(n):
    return [pl.BlockSpec(memory_space=pltpu.VMEM)] * n


SMEM = pl.BlockSpec(memory_space=pltpu.SMEM)
COST = pl.CostEstimate(flops=1, bytes_accessed=1, transcendentals=0)


def params(*arrays):
    held = sum(math.prod(a.shape) * a.dtype.itemsize for a in arrays)
    return pltpu.CompilerParams(vmem_limit_bytes=held + 8 * 1024 * 1024)


def after(value, *others):
    return lax.optimization_barrier((value,) + others)[0]


def hop(axis, size, step):
    pairs = [(i, i ^ step) for i in range(size)]
    return lambda x: lax.ppermute(x, axis, pairs)


def per_device(points, cluster_of, subcentroids):
    count, width = points.shape
    owners = lax.axis_size("own")
    helpers = lax.axis_size("hlp")
    depth = min(count // 2, 4 * count // owners)
    share_rows = subcentroids.shape[1]
    subs = share_rows * helpers
    groups = min(GROUPS, owners)
    per = owners // groups
    height = per * depth

    me = lax.axis_index("own").astype(jnp.int32).reshape(1)
    helper = lax.axis_index("hlp").astype(jnp.int32).reshape(1)
    cluster = cluster_of.reshape(1, count)

    blocks = [jax.ShapeDtypeStruct((height, width), BF)] * groups
    packed = pl.pallas_call(
        functools.partial(pack_kernel, depth, owners),
        out_shape=blocks,
        in_specs=[SMEM] + vmem(2),
        out_specs=vmem(groups),
        compiler_params=params(points, *blocks),
        cost_estimate=COST,
        name="pack",
    )(me, cluster, points)

    def across(block, g):
        done = []
        for j in range(per):
            step = g * per + j
            piece = block if per == 1 else block[j * depth : (j + 1) * depth]
            done.append(piece if step == 0 else hop("own", owners, step)(piece))
        return joined(done)

    def over_chips(block):
        return [block] + [hop("hlp", helpers, step)(block) for step in range(2, helpers, 2)]

    def over_cores(held):
        return [x for block in held for x in (block, hop("hlp", helpers, 1)(block))]

    state = [jax.ShapeDtypeStruct((subs, width), F32), jax.ShapeDtypeStruct((subs, 128), F32)]
    moved = [across(packed[g], g) for g in range(groups)]
    held = [over_chips(block) for block in moved]
    start = over_cores(over_chips(after(subcentroids[0], *held[0])))
    soon = groups // 2
    earlier = [r for part in held[:soon] for r in over_cores(part)]
    shares = jax.ShapeDtypeStruct((len(earlier) * height, subs), BF)
    sums, mass = pl.pallas_call(
        functools.partial(first_kernel, helpers),
        out_shape=state,
        in_specs=vmem(len(start) + len(earlier)),
        out_specs=vmem(2),
        scratch_shapes=[pltpu.VMEM(shares.shape, BF)],
        compiler_params=params(*start, *earlier, *state, shares),
        cost_estimate=COST,
        name="first_rows",
    )(*start, *earlier)
    late = [r for part in held[soon:-1] for r in over_cores(part)]
    late += over_cores(held[-1][:-1] + [after(held[-1][-1], sums)])
    logs = [jax.ShapeDtypeStruct((height, subs), BF)] * groups
    refined = jax.ShapeDtypeStruct((share_rows, width), F32)
    total = (len(earlier) + len(late)) * height
    scratch = state + [
        jax.ShapeDtypeStruct((subs, width), BF),
        jax.ShapeDtypeStruct((total, subs), BF),
        jax.ShapeDtypeStruct((total, width), BF),
    ]
    refined, *logs = pl.pallas_call(
        functools.partial(last_kernel, helpers, (len(earlier), len(late), groups), share_rows),
        out_shape=[refined] + logs,
        in_specs=[SMEM]
        + vmem(2 + helpers)
        + [pl.BlockSpec(memory_space=pl.ANY)] * (len(earlier) + len(late)),
        out_specs=vmem(1 + groups),
        scratch_shapes=[pltpu.VMEM(s.shape, s.dtype) for s in scratch]
        + [pltpu.SemaphoreType.DMA((len(earlier) + len(late),))],
        compiler_params=params(*start, *state, *scratch, refined, *logs),
        cost_estimate=COST,
        name="rounds",
    )(helper, *start, sums, mass, *earlier, *late)

    back = [across(logs[g], g) for g in range(groups)]
    out = jax.ShapeDtypeStruct((count, subs), F32)
    log_resp = pl.pallas_call(
        functools.partial(unpack_kernel, depth, owners),
        out_shape=out,
        in_specs=[SMEM] + vmem(1 + groups),
        out_specs=pl.BlockSpec(memory_space=pltpu.VMEM),
        compiler_params=params(*back, out),
        cost_estimate=COST,
        name="unpack",
    )(me, cluster, *back)
    return (refined[None], log_resp)


def solution(mesh):
    in_specs = (
        P(("grp", "own", "hlp"), None),
        P(("grp", "own", "hlp")),
        P(("grp", "own"), "hlp", None),
    )
    out_specs = (P(("grp", "own"), "hlp", None), P(("grp", "own", "hlp"), None))
    return jax.shard_map(
        per_device, mesh=mesh, in_specs=in_specs, out_specs=out_specs, check_vma=False
    )
```

```python
import functools
import math

import jax
import jax.numpy as jnp
from jax import lax
from jax.experimental import pallas as pl
from jax.experimental.pallas import tpu as pltpu
from jax.sharding import PartitionSpec as P

ITERS = 2
GROUPS = 4
TILE = 256

smoothing_factor = 16.0
prior_count = 1.0

EMPTY = 64.0
LIMIT = 32.0

BF = jnp.bfloat16
F32 = jnp.float32
TN = (((0,), (0,)), ((), ()))
NN = (((1,), (0,)), ((), ()))


def matmul(a, b, dims):
    return lax.dot_general(a, b, dims, preferred_element_type=F32)


def slots_of(me, cluster, depth, owners):
    count = cluster.shape[1]
    height = max(16, owners)
    offset = jnp.bitwise_xor(cluster, me)
    member = lax.broadcasted_iota(jnp.int32, (height, count), 0) == offset
    earlier = lax.broadcasted_iota(jnp.int32, (count, count), 0) < lax.broadcasted_iota(
        jnp.int32, (count, count), 1
    )
    member = jnp.where(member, 1.0, 0.0)
    before = matmul(member.astype(BF), jnp.where(earlier, 1.0, 0.0).astype(BF), NN)
    rank = jnp.sum(before * member, axis=0, keepdims=True).astype(jnp.int32)
    return offset * depth + rank, jnp.sum(member, axis=1, keepdims=True)


def fetch(refs, target, arrived):
    height = refs[0].shape[0]
    copies = [
        pltpu.make_async_copy(ref, target.at[i * height : (i + 1) * height], arrived.at[i])
        for i, ref in enumerate(refs)
    ]
    for copy in copies:
        copy.start()
    return copies


def settle(copies):
    for copy in copies:
        copy.wait()


def pack_kernel(depth, owners, me_ref, cluster_hbm, points_hbm, centres_hbm, *refs):
    *outs, cluster_ref, points_ref, arrived = refs
    names = pltpu.make_async_copy(cluster_hbm, cluster_ref, arrived.at[1])
    names.start()
    points = fetch([points_hbm], points_ref, arrived)
    height = outs[-1].shape[0]
    centres = fetch([centres_hbm], outs[0].at[height:], arrived.at[2:])
    names.wait()
    slot, tally = slots_of(me_ref[0], cluster_ref[...], depth, owners)
    settle(points)
    points = points_ref[...]
    per = height // depth
    for g, out in enumerate(outs):
        rows = lax.broadcasted_iota(jnp.int32, (height, points.shape[0]), 0) + g * height
        pick = jnp.where(rows == slot, 1.0, 0.0).astype(BF)
        block = matmul(pick, points, NN)
        for j in range(per):
            held = tally[g * per + j : g * per + j + 1, :].astype(jnp.int32)
            local = lax.broadcasted_iota(jnp.int32, (depth, 1), 0)
            part = block[j * depth : (j + 1) * depth]
            out[j * depth : (j + 1) * depth, :] = jnp.where(local < held, part, EMPTY).astype(BF)
    settle(centres)


def unpack_kernel(depth, owners, me_ref, cluster_ref, *refs):
    *logs, out = refs
    slot, _ = slots_of(me_ref[0], cluster_ref[...], depth, owners)
    count = slot.shape[1]
    column = jnp.broadcast_to(slot.astype(F32), (128, count)).T[:, 0:1].astype(jnp.int32)
    height = logs[0].shape[0]
    total = None
    for g, block in enumerate(logs):
        lanes = lax.broadcasted_iota(jnp.int32, (count, height), 1) + g * height
        pick = jnp.where(lanes == column, 1.0, 0.0).astype(BF)
        term = matmul(pick, block[...], NN)
        total = term if total is None else total + term
    out[...] = total


def square_norms(centres):
    wide = centres.astype(F32)
    column = jnp.sum(wide * wide, axis=1, keepdims=True)
    return jnp.broadcast_to(column, (column.shape[0], 128)).T[0:1]


def joined(parts):
    return parts[0] if len(parts) == 1 else jnp.concatenate(parts, axis=0)


def energies(turned, norms, rows):
    return matmul(rows, turned, NN) * (2.0 / smoothing_factor) - norms * (1.0 / smoothing_factor)


def accumulate(turned, norms, tiles, share_ref, state_ref, fresh):
    start = 0
    for rows in tiles:
        logits = energies(turned, norms, rows)
        top = jnp.max(logits, axis=1, keepdims=True)
        weight = jnp.exp(logits - top)
        live = jnp.where(rows[:, 0:1].astype(F32) < LIMIT, 1.0, 0.0)
        scale = live / jnp.sum(weight, axis=1, keepdims=True)
        share_ref[start : start + rows.shape[0], :] = (weight * scale).astype(BF)
        start += rows.shape[0]
    width = state_ref.shape[1] - 128
    start = 0
    for i, rows in enumerate(tiles):
        share = share_ref[start : start + rows.shape[0], :]
        mass = matmul(share, jnp.ones((rows.shape[0], 128), BF), TN)
        part = matmul(share, rows, TN)
        if fresh and i == 0:
            state_ref[:, width:] = mass
            state_ref[:, :width] = part
        else:
            state_ref[:, width:] += mass
            state_ref[:, :width] += part
        start += rows.shape[0]


def tiles_of(rows, first, last):
    return [rows[r : r + TILE, :] for r in range(first, last, TILE)]


def some_kernel(helpers, height, *refs):
    *given, out, state_ref, centres_ref, share_ref, rows, arrived, ready, kept = refs
    centres = fetch([ref.at[height:] for ref in given[:helpers]], centres_ref, ready)
    copies = fetch([ref.at[:height] for ref in given], rows, arrived)
    settle(centres)
    centres = centres_ref[...]
    norms = square_norms(centres)
    turned = centres.T
    settle(copies)
    accumulate(turned, norms, tiles_of(rows, 0, rows.shape[0]), share_ref, state_ref, True)
    settle(fetch([state_ref], out, kept))


def refine(centres, state_ref):
    width = centres.shape[1]
    mass = state_ref[:, width : width + 1]
    return (state_ref[:, :width] + prior_count * centres.astype(F32)) / (mass + prior_count)


def last_kernel(helpers, counts, share_rows, helper_ref, *refs):
    earlier, late, own = counts
    old, refs = refs[:1], refs[1:]
    given, refs = refs[: earlier + late], refs[earlier + late :]
    refined_ref, logs, refs = refs[0], refs[1 : 1 + own], refs[1 + own :]
    state_ref, ordered, share_ref, rows, arrived, ready, kept = refs
    height = given[-1].shape[0]
    held = earlier * height
    centres = fetch([ref.at[height:] for ref in given[:helpers]], ordered, ready)
    given = [ref.at[:height] for ref in given]
    later = fetch(given[earlier:], rows.at[held:], arrived.at[earlier:])
    sooner = fetch(given[:earlier], rows, arrived)
    state = fetch(old, state_ref, kept)
    helper = helper_ref[0]
    settle(centres)
    centres = ordered[...]
    norms = square_norms(centres)
    turned = centres.T
    settle(later + state)
    accumulate(turned, norms, tiles_of(rows, held, rows.shape[0]), share_ref, state_ref, False)
    settle(sooner)
    for turn in range(1, ITERS):
        centres = refine(centres, state_ref).astype(BF)
        norms = square_norms(centres)
        turned = centres.T
        accumulate(turned, norms, tiles_of(rows, 0, rows.shape[0]), share_ref, state_ref, True)
    refined = refine(centres, state_ref)
    refined_ref[...] = refined[0:share_rows]
    centres = refined.astype(BF)
    for j in range(helpers):
        place = pl.multiple_of(jnp.bitwise_xor(helper, j) * share_rows, share_rows)
        ordered[pl.ds(place, share_rows), :] = centres[j * share_rows : (j + 1) * share_rows]
    centres = ordered[...]
    norms = square_norms(centres)
    turned = centres.T
    for i, out in enumerate(logs):
        first = i * helpers * height
        logits = energies(turned, norms, rows[first : first + height, :])
        top = jnp.max(logits, axis=1, keepdims=True)
        total = jnp.log(jnp.sum(jnp.exp(logits - top), axis=1, keepdims=True))
        out[...] = (logits - (top + total)).astype(BF)


def vmem(n):
    return [pl.BlockSpec(memory_space=pltpu.VMEM)] * n


SMEM = pl.BlockSpec(memory_space=pltpu.SMEM)
HBM = pl.BlockSpec(memory_space=pltpu.HBM)
COST = pl.CostEstimate(flops=1, bytes_accessed=1, transcendentals=0)


def params(*arrays):
    held = sum(math.prod(a.shape) * a.dtype.itemsize for a in arrays)
    return pltpu.CompilerParams(vmem_limit_bytes=held + 8 * 1024 * 1024)


def in_hbm(value):
    return pltpu.with_memory_space_constraint(value, pltpu.HBM)


def after(value, *others):
    return lax.optimization_barrier((value,) + others)[0]


def hop(axis, size, step):
    pairs = [(i, i ^ step) for i in range(size)]
    return lambda x: lax.ppermute(x, axis, pairs)


def per_device(points, cluster_of, subcentroids):
    count, width = points.shape
    owners = lax.axis_size("own")
    helpers = lax.axis_size("hlp")
    depth = min(count // 2, 4 * count // owners)
    share_rows = subcentroids.shape[1]
    subs = share_rows * helpers
    groups = min(GROUPS, owners)
    per = owners // groups
    height = per * depth

    me = lax.axis_index("own").astype(jnp.int32).reshape(1)
    helper = lax.axis_index("hlp").astype(jnp.int32).reshape(1)
    cluster = cluster_of.reshape(1, count)

    blocks = [jax.ShapeDtypeStruct((height + (0 if g else share_rows), width), BF) for g in range(groups)]
    packed = pl.pallas_call(
        functools.partial(pack_kernel, depth, owners),
        out_shape=blocks,
        in_specs=[SMEM] + [HBM] * 3,
        out_specs=vmem(groups),
        scratch_shapes=[
            pltpu.VMEM(cluster.shape, jnp.int32),
            pltpu.VMEM(points.shape, BF),
            pltpu.SemaphoreType.DMA((3,)),
        ],
        compiler_params=params(points, *blocks),
        cost_estimate=COST,
        name="pack",
    )(me, in_hbm(cluster), in_hbm(points), in_hbm(subcentroids[0]))

    def across(block, g):
        if per == 1:
            return hop("own", owners, g)(block) if g else block
        done = []
        for j in range(per):
            step = g * per + j
            piece = block[j * depth : (j + 1) * depth]
            done.append(hop("own", owners, step)(piece) if step else piece)
        if block.shape[0] > height:
            done.append(block[height:])
        return joined(done)

    def over_chips(block):
        return [block] + [hop("hlp", helpers, step)(block) for step in range(2, helpers, 2)]

    def over_cores(held):
        return [x for block in held for x in (block, hop("hlp", helpers, 1)(block))]

    state = jax.ShapeDtypeStruct((subs, width + 128), F32)
    centre_table = jax.ShapeDtypeStruct((subs, width), BF)

    def scratch(n):
        return [
            state,
            centre_table,
            jax.ShapeDtypeStruct((n * height, subs), BF),
            jax.ShapeDtypeStruct((n * height, width), BF),
        ]

    def semaphores(*counts):
        return [pltpu.SemaphoreType.DMA((n,)) for n in counts]

    beside = hop("hlp", helpers, 1)
    moved = [packed[0]]
    for g in range(1, groups - 1):
        moved.append(across(packed[g], g))
    moved.append(across(after(packed[-1], moved[-1]) if groups > 1 else packed[-1], groups - 1))
    held = [over_chips(block) for block in moved]
    own_beside = beside(after(packed[0], held[0][1]))
    rows = [[moved[0], own_beside] + over_cores(held[0][1:])] + [over_cores(part) for part in held[1:-1]]
    given = [r for part in rows for r in part]
    own = scratch(len(given))
    sofar = pl.pallas_call(
        functools.partial(some_kernel, helpers, height),
        out_shape=state,
        in_specs=[HBM] * len(given),
        out_specs=HBM,
        scratch_shapes=[pltpu.VMEM(s.shape, s.dtype) for s in own] + semaphores(len(given), helpers, 1),
        compiler_params=params(*own),
        cost_estimate=COST,
        name="some_rows",
    )(*given)
    late = over_cores(held[-1][:-1] + [after(held[-1][-1], sofar)])
    earlier = [r for part in rows for r in part]
    logs = [jax.ShapeDtypeStruct((height, subs), BF)] * groups
    refined = jax.ShapeDtypeStruct((share_rows, width), F32)
    own = scratch(len(earlier) + len(late))
    refined, *logs = pl.pallas_call(
        functools.partial(last_kernel, helpers, (len(earlier), len(late), groups), share_rows),
        out_shape=[refined] + logs,
        in_specs=[SMEM] + [HBM] * (1 + len(earlier) + len(late)),
        out_specs=vmem(1 + groups),
        scratch_shapes=[pltpu.VMEM(s.shape, s.dtype) for s in own]
        + semaphores(len(earlier) + len(late), helpers, 1),
        compiler_params=params(*own, refined, *logs),
        cost_estimate=COST,
        name="rounds",
    )(helper, sofar, *[in_hbm(r) for r in earlier + late])

    back = [across(logs[g], g) for g in range(groups)]
    out = jax.ShapeDtypeStruct((count, subs), F32)
    log_resp = pl.pallas_call(
        functools.partial(unpack_kernel, depth, owners),
        out_shape=out,
        in_specs=[SMEM] + vmem(1 + groups),
        out_specs=pl.BlockSpec(memory_space=pltpu.VMEM),
        compiler_params=params(*back, out),
        cost_estimate=COST,
        name="unpack",
    )(me, cluster, *back)
    return (refined[None], log_resp)


def solution(mesh):
    in_specs = (
        P(("grp", "own", "hlp"), None),
        P(("grp", "own", "hlp")),
        P(("grp", "own"), "hlp", None),
    )
    out_specs = (P(("grp", "own"), "hlp", None), P(("grp", "own", "hlp"), None))
    return jax.shard_map(
        per_device, mesh=mesh, in_specs=in_specs, out_specs=out_specs, check_vma=False
    )
```

```python
import functools
import math

import jax
import jax.numpy as jnp
from jax import lax
from jax.experimental import pallas as pl
from jax.experimental.pallas import tpu as pltpu
from jax.sharding import PartitionSpec as P

ITERS = 2
GROUPS = 4
TILE = 256

smoothing_factor = 16.0
prior_count = 1.0

EMPTY = 64.0
LIMIT = 32.0

BF = jnp.bfloat16
F32 = jnp.float32
TN = (((0,), (0,)), ((), ()))
NN = (((1,), (0,)), ((), ()))


def matmul(a, b, dims):
    return lax.dot_general(a, b, dims, preferred_element_type=F32)


def slots_of(me, cluster, depth, owners):
    count = cluster.shape[1]
    height = max(16, owners)
    offset = jnp.bitwise_xor(cluster, me)
    member = lax.broadcasted_iota(jnp.int32, (height, count), 0) == offset
    earlier = lax.broadcasted_iota(jnp.int32, (count, count), 0) < lax.broadcasted_iota(
        jnp.int32, (count, count), 1
    )
    member = jnp.where(member, 1.0, 0.0)
    before = matmul(member.astype(BF), jnp.where(earlier, 1.0, 0.0).astype(BF), NN)
    rank = jnp.sum(before * member, axis=0, keepdims=True).astype(jnp.int32)
    return offset * depth + rank, jnp.sum(member, axis=1, keepdims=True)


def fetch(refs, target, arrived):
    height = refs[0].shape[0]
    copies = [
        pltpu.make_async_copy(ref, target.at[i * height : (i + 1) * height], arrived.at[i])
        for i, ref in enumerate(refs)
    ]
    for copy in copies:
        copy.start()
    return copies


def settle(copies):
    for copy in copies:
        copy.wait()


def pack_kernel(depth, owners, me_ref, cluster_hbm, points_hbm, centres_hbm, *refs):
    *outs, cluster_ref, points_ref, arrived = refs
    names = pltpu.make_async_copy(cluster_hbm, cluster_ref, arrived.at[1])
    names.start()
    points = fetch([points_hbm], points_ref, arrived)
    height = outs[-1].shape[0]
    centres = fetch([centres_hbm], outs[0].at[height:], arrived.at[2:])
    names.wait()
    slot, tally = slots_of(me_ref[0], cluster_ref[...], depth, owners)
    settle(points)
    points = points_ref[...]
    per = height // depth
    for g, out in enumerate(outs):
        rows = lax.broadcasted_iota(jnp.int32, (height, points.shape[0]), 0) + g * height
        pick = jnp.where(rows == slot, 1.0, 0.0).astype(BF)
        block = matmul(pick, points, NN)
        for j in range(per):
            held = tally[g * per + j : g * per + j + 1, :].astype(jnp.int32)
            local = lax.broadcasted_iota(jnp.int32, (depth, 1), 0)
            part = block[j * depth : (j + 1) * depth]
            out[j * depth : (j + 1) * depth, :] = jnp.where(local < held, part, EMPTY).astype(BF)
    settle(centres)


def unpack_kernel(depth, owners, me_ref, cluster_ref, *refs):
    *logs, out = refs
    logs = logs[::-1]
    slot, _ = slots_of(me_ref[0], cluster_ref[...], depth, owners)
    count = slot.shape[1]
    column = jnp.broadcast_to(slot.astype(F32), (128, count)).T[:, 0:1].astype(jnp.int32)
    height = logs[0].shape[0]
    total = None
    for g, block in enumerate(logs):
        lanes = lax.broadcasted_iota(jnp.int32, (count, height), 1) + g * height
        pick = jnp.where(lanes == column, 1.0, 0.0).astype(BF)
        term = matmul(pick, block[...], NN)
        total = term if total is None else total + term
    out[...] = total


def square_norms(centres):
    wide = centres.astype(F32)
    column = jnp.sum(wide * wide, axis=1, keepdims=True)
    return jnp.broadcast_to(column, (column.shape[0], 128)).T[0:1]


def joined(parts):
    return parts[0] if len(parts) == 1 else jnp.concatenate(parts, axis=0)


def energies(turned, norms, rows):
    return matmul(rows, turned, NN) * (2.0 / smoothing_factor) - norms * (1.0 / smoothing_factor)


def accumulate(turned, norms, tiles, share_ref, state_ref, fresh):
    start = 0
    for rows in tiles:
        logits = energies(turned, norms, rows)
        top = jnp.max(logits, axis=1, keepdims=True)
        weight = jnp.exp(logits - top)
        live = jnp.where(rows[:, 0:1].astype(F32) < LIMIT, 1.0, 0.0)
        scale = live / jnp.sum(weight, axis=1, keepdims=True)
        share_ref[start : start + rows.shape[0], :] = (weight * scale).astype(BF)
        start += rows.shape[0]
    width = state_ref.shape[1] - 128
    start = 0
    for i, rows in enumerate(tiles):
        share = share_ref[start : start + rows.shape[0], :]
        mass = matmul(share, jnp.ones((rows.shape[0], 128), BF), TN)
        part = matmul(share, rows, TN)
        if fresh and i == 0:
            state_ref[:, width:] = mass
            state_ref[:, :width] = part
        else:
            state_ref[:, width:] += mass
            state_ref[:, :width] += part
        start += rows.shape[0]


def tiles_of(rows, first, last):
    return [rows[r : r + TILE, :] for r in range(first, last, TILE)]


def some_kernel(helpers, height, *refs):
    *given, out, state_ref, centres_ref, share_ref, rows, arrived, ready, kept = refs
    centres = fetch([ref.at[height:] for ref in given[:helpers]], centres_ref, ready)
    copies = fetch([ref.at[:height] for ref in given], rows, arrived)
    settle(centres)
    centres = centres_ref[...]
    norms = square_norms(centres)
    turned = centres.T
    settle(copies)
    accumulate(turned, norms, tiles_of(rows, 0, rows.shape[0]), share_ref, state_ref, True)
    settle(fetch([state_ref], out, kept))


def refine(centres, state_ref):
    width = centres.shape[1]
    mass = state_ref[:, width : width + 1]
    return (state_ref[:, :width] + prior_count * centres.astype(F32)) / (mass + prior_count)


def last_kernel(helpers, counts, share_rows, helper_ref, *refs):
    earlier, late, own = counts
    old, refs = refs[:1], refs[1:]
    given, refs = refs[: earlier + late], refs[earlier + late :]
    refined_ref, logs, refs = refs[0], refs[1 : 1 + own], refs[1 + own :]
    state_ref, ordered, share_ref, rows, arrived, ready, kept = refs
    height = given[-1].shape[0]
    held = earlier * height
    centres = fetch([ref.at[height:] for ref in given[:helpers]], ordered, ready)
    given = [ref.at[:height] for ref in given]
    later = fetch(given[earlier:], rows.at[held:], arrived.at[earlier:])
    state = fetch(old, state_ref, kept)
    sooner = fetch(given[:earlier], rows, arrived)
    helper = helper_ref[0]
    settle(centres)
    centres = ordered[...]
    norms = square_norms(centres)
    turned = centres.T
    settle(later + state)
    accumulate(turned, norms, tiles_of(rows, held, rows.shape[0]), share_ref, state_ref, False)
    settle(sooner)
    for turn in range(1, ITERS):
        centres = refine(centres, state_ref).astype(BF)
        norms = square_norms(centres)
        turned = centres.T
        accumulate(turned, norms, tiles_of(rows, 0, rows.shape[0]), share_ref, state_ref, True)
    refined = refine(centres, state_ref)
    refined_ref[...] = refined[0:share_rows]
    centres = refined.astype(BF)
    for j in range(helpers):
        place = pl.multiple_of(jnp.bitwise_xor(helper, j) * share_rows, share_rows)
        ordered[pl.ds(place, share_rows), :] = centres[j * share_rows : (j + 1) * share_rows]
    centres = ordered[...]
    norms = square_norms(centres)
    turned = centres.T
    own_rows = [rows[g * helpers * height : g * helpers * height + height, :] for g in range(own)]
    pair = 2 if 2 * height <= TILE and own % 2 == 0 else 1
    for g in range(0, own, pair):
        logits = energies(turned, norms, joined(own_rows[g : g + pair]))
        top = jnp.max(logits, axis=1, keepdims=True)
        total = jnp.log(jnp.sum(jnp.exp(logits - top), axis=1, keepdims=True))
        result = (logits - (top + total)).astype(BF)
        for i in range(pair):
            logs[g + i][...] = result[i * height : (i + 1) * height]


def vmem(n):
    return [pl.BlockSpec(memory_space=pltpu.VMEM)] * n


SMEM = pl.BlockSpec(memory_space=pltpu.SMEM)
HBM = pl.BlockSpec(memory_space=pltpu.HBM)
COST = pl.CostEstimate(flops=1, bytes_accessed=1, transcendentals=0)


def params(*arrays):
    held = sum(math.prod(a.shape) * a.dtype.itemsize for a in arrays)
    return pltpu.CompilerParams(vmem_limit_bytes=held + 8 * 1024 * 1024)


def in_hbm(value):
    return pltpu.with_memory_space_constraint(value, pltpu.HBM)


def after(value, *others):
    return lax.optimization_barrier((value,) + others)[0]


def hop(axis, size, step):
    pairs = [(i, i ^ step) for i in range(size)]
    return lambda x: lax.ppermute(x, axis, pairs)


def per_device(points, cluster_of, subcentroids):
    count, width = points.shape
    owners = lax.axis_size("own")
    helpers = lax.axis_size("hlp")
    depth = min(count // 2, 4 * count // owners)
    share_rows = subcentroids.shape[1]
    subs = share_rows * helpers
    groups = min(GROUPS, owners)
    per = owners // groups
    height = per * depth

    me = lax.axis_index("own").astype(jnp.int32).reshape(1)
    helper = lax.axis_index("hlp").astype(jnp.int32).reshape(1)
    cluster = cluster_of.reshape(1, count)

    blocks = [jax.ShapeDtypeStruct((height + (0 if g else share_rows), width), BF) for g in range(groups)]
    packed = pl.pallas_call(
        functools.partial(pack_kernel, depth, owners),
        out_shape=blocks,
        in_specs=[SMEM] + [HBM] * 3,
        out_specs=vmem(groups),
        scratch_shapes=[
            pltpu.VMEM(cluster.shape, jnp.int32),
            pltpu.VMEM(points.shape, BF),
            pltpu.SemaphoreType.DMA((3,)),
        ],
        compiler_params=params(points, *blocks),
        cost_estimate=COST,
        name="pack",
    )(me, in_hbm(cluster), in_hbm(points), in_hbm(subcentroids[0]))

    def across(block, g):
        if per == 1:
            return hop("own", owners, g)(block) if g else block
        done = []
        for j in range(per):
            step = g * per + j
            piece = block[j * depth : (j + 1) * depth]
            done.append(hop("own", owners, step)(piece) if step else piece)
        if block.shape[0] > height:
            done.append(block[height:])
        return joined(done)

    def over_chips(block):
        return [block] + [hop("hlp", helpers, step)(block) for step in range(2, helpers, 2)]

    def over_cores(held):
        return [x for block in held for x in (block, hop("hlp", helpers, 1)(block))]

    state = jax.ShapeDtypeStruct((subs, width + 128), F32)
    centre_table = jax.ShapeDtypeStruct((subs, width), BF)

    def scratch(n):
        return [
            state,
            centre_table,
            jax.ShapeDtypeStruct((n * height, subs), BF),
            jax.ShapeDtypeStruct((n * height, width), BF),
        ]

    def semaphores(*counts):
        return [pltpu.SemaphoreType.DMA((n,)) for n in counts]

    beside = hop("hlp", helpers, 1)
    moved = [packed[0]]
    for g in range(1, groups - 1):
        moved.append(across(packed[g], g))
    moved.append(across(after(packed[-1], moved[-1]) if groups > 1 else packed[-1], groups - 1))
    held = [over_chips(block) for block in moved]
    own_beside = beside(after(packed[0], held[0][1]))
    rows = [[moved[0], own_beside] + over_cores(held[0][1:])] + [over_cores(part) for part in held[1:-1]]
    given = [r for part in rows for r in part] + over_cores(held[-1][:1])
    own = scratch(len(given))
    sofar = pl.pallas_call(
        functools.partial(some_kernel, helpers, height),
        out_shape=state,
        in_specs=[HBM] * len(given),
        out_specs=HBM,
        scratch_shapes=[pltpu.VMEM(s.shape, s.dtype) for s in own] + semaphores(len(given), helpers, 1),
        compiler_params=params(*own),
        cost_estimate=COST,
        name="some_rows",
    )(*given)
    late = over_cores(held[-1][1:-1] + [after(held[-1][-1], sofar)])
    earlier = given
    logs = [jax.ShapeDtypeStruct((height, subs), BF)] * groups
    refined = jax.ShapeDtypeStruct((share_rows, width), F32)
    own = scratch(len(earlier) + len(late))
    refined, *logs = pl.pallas_call(
        functools.partial(last_kernel, helpers, (len(earlier), len(late), groups), share_rows),
        out_shape=[refined] + logs,
        in_specs=[SMEM] + [HBM] * (1 + len(earlier) + len(late)),
        out_specs=vmem(1 + groups),
        scratch_shapes=[pltpu.VMEM(s.shape, s.dtype) for s in own]
        + semaphores(len(earlier) + len(late), helpers, 1),
        compiler_params=params(*own, refined, *logs),
        cost_estimate=COST,
        name="rounds",
    )(helper, sofar, *[in_hbm(r) for r in earlier], *late)

    back = [across(logs[g], g) for g in reversed(range(groups))]
    out = jax.ShapeDtypeStruct((count, subs), F32)
    log_resp = pl.pallas_call(
        functools.partial(unpack_kernel, depth, owners),
        out_shape=out,
        in_specs=[SMEM] + vmem(1 + groups),
        out_specs=pl.BlockSpec(memory_space=pltpu.VMEM),
        compiler_params=params(*back, out),
        cost_estimate=COST,
        name="unpack",
    )(me, cluster, *back)
    return (refined[None], log_resp)


def solution(mesh):
    in_specs = (
        P(("grp", "own", "hlp"), None),
        P(("grp", "own", "hlp")),
        P(("grp", "own"), "hlp", None),
    )
    out_specs = (P(("grp", "own"), "hlp", None), P(("grp", "own", "hlp"), None))
    return jax.shard_map(
        per_device, mesh=mesh, in_specs=in_specs, out_specs=out_specs, check_vma=False
    )
```

```python
import functools
import math

import jax
import jax.numpy as jnp
from jax import lax
from jax.experimental import pallas as pl
from jax.experimental.pallas import tpu as pltpu
from jax.sharding import PartitionSpec as P

ITERS = 2
GROUPS = 4
TILE = 256

smoothing_factor = 16.0
prior_count = 1.0

EMPTY = 64.0
LIMIT = 32.0

BF = jnp.bfloat16
F32 = jnp.float32
TN = (((0,), (0,)), ((), ()))
NN = (((1,), (0,)), ((), ()))


def matmul(a, b, dims):
    return lax.dot_general(a, b, dims, preferred_element_type=F32)


def precedes(count):
    earlier = lax.broadcasted_iota(jnp.int32, (count, count), 0) < lax.broadcasted_iota(
        jnp.int32, (count, count), 1
    )
    return jnp.where(earlier, 1.0, 0.0).astype(BF)


def slots_of(cluster, earlier, depth, owners):
    count = cluster.shape[1]
    height = max(16, owners)
    offset = jnp.bitwise_xor(cluster, lax.axis_index("own").astype(jnp.int32))
    member = lax.broadcasted_iota(jnp.int32, (height, count), 0) == offset
    member = jnp.where(member, 1.0, 0.0)
    before = matmul(member.astype(BF), earlier, NN)
    rank = jnp.sum(before * member, axis=0, keepdims=True).astype(jnp.int32)
    return offset * depth + rank, jnp.sum(member, axis=1, keepdims=True)


def fetch(refs, target, arrived):
    height = refs[0].shape[0]
    copies = [
        pltpu.make_async_copy(ref, target.at[i * height : (i + 1) * height], arrived.at[i])
        for i, ref in enumerate(refs)
    ]
    for copy in copies:
        copy.start()
    return copies


def settle(copies):
    for copy in copies:
        copy.wait()


def pack_kernel(depth, owners, cluster_hbm, points_hbm, centres_hbm, *refs):
    *outs, cluster_ref, points_ref, arrived = refs
    names = pltpu.make_async_copy(cluster_hbm, cluster_ref, arrived.at[1])
    names.start()
    points = fetch([points_hbm], points_ref, arrived)
    height = outs[-1].shape[0]
    centres = fetch([centres_hbm], outs[0].at[height:], arrived.at[2:])
    earlier = precedes(cluster_ref.shape[1])
    names.wait()
    slot, tally = slots_of(cluster_ref[...], earlier, depth, owners)
    settle(points)
    points = points_ref[...]
    per = height // depth
    for g, out in enumerate(outs):
        rows = lax.broadcasted_iota(jnp.int32, (height, points.shape[0]), 0) + g * height
        pick = jnp.where(rows == slot, 1.0, 0.0).astype(BF)
        block = matmul(pick, points, NN)
        for j in range(per):
            held = tally[g * per + j : g * per + j + 1, :].astype(jnp.int32)
            local = lax.broadcasted_iota(jnp.int32, (depth, 1), 0)
            part = block[j * depth : (j + 1) * depth]
            out[j * depth : (j + 1) * depth, :] = jnp.where(local < held, part, EMPTY).astype(BF)
    settle(centres)


def places_kernel(depth, owners, cluster_ref, out):
    count, slots = out.shape
    slot, _ = slots_of(cluster_ref[...], precedes(count), depth, owners)
    column = jnp.broadcast_to(slot.astype(F32), (128, count)).T[:, 0:1].astype(jnp.int32)
    lanes = lax.broadcasted_iota(jnp.int32, (count, slots), 1)
    out[...] = jnp.where(lanes == column, 1.0, 0.0).astype(BF)


def unpack_kernel(places_ref, *refs):
    *logs, out = refs
    height = logs[0].shape[0]
    total = None
    for g, block in enumerate(logs[::-1]):
        term = matmul(places_ref[:, g * height : (g + 1) * height], block[...], NN)
        total = term if total is None else total + term
    out[...] = total


def square_norms(centres):
    wide = centres.astype(F32)
    column = jnp.sum(wide * wide, axis=1, keepdims=True)
    return jnp.broadcast_to(column, (column.shape[0], 128)).T[0:1]


def joined(parts):
    return parts[0] if len(parts) == 1 else jnp.concatenate(parts, axis=0)


def energies(turned, norms, rows):
    return matmul(rows, turned, NN) * (2.0 / smoothing_factor) - norms * (1.0 / smoothing_factor)


def accumulate(turned, norms, tiles, share_ref, state_ref, fresh):
    start = 0
    for rows in tiles:
        logits = energies(turned, norms, rows)
        top = jnp.max(logits, axis=1, keepdims=True)
        weight = jnp.exp(logits - top)
        live = jnp.where(rows[:, 0:1].astype(F32) < LIMIT, 1.0, 0.0)
        scale = live / jnp.sum(weight, axis=1, keepdims=True)
        share_ref[start : start + rows.shape[0], :] = (weight * scale).astype(BF)
        start += rows.shape[0]
    width = state_ref.shape[1] - 128
    start = 0
    for i, rows in enumerate(tiles):
        share = share_ref[start : start + rows.shape[0], :]
        mass = matmul(share, jnp.ones((rows.shape[0], 128), BF), TN)
        part = matmul(share, rows, TN)
        if fresh and i == 0:
            state_ref[:, width:] = mass
            state_ref[:, :width] = part
        else:
            state_ref[:, width:] += mass
            state_ref[:, :width] += part
        start += rows.shape[0]


def tiles_of(rows, first, last):
    return [rows[r : r + TILE, :] for r in range(first, last, TILE)]


def some_kernel(helpers, height, *refs):
    *given, out, state_ref, centres_ref, share_ref, rows, arrived, ready, kept = refs
    centres = fetch([ref.at[height:] for ref in given[:helpers]], centres_ref, ready)
    copies = fetch([ref.at[:height] for ref in given], rows, arrived)
    settle(centres)
    centres = centres_ref[...]
    norms = square_norms(centres)
    turned = centres.T
    settle(copies)
    accumulate(turned, norms, tiles_of(rows, 0, rows.shape[0]), share_ref, state_ref, True)
    settle(fetch([state_ref], out, kept))


def refine(centres, *states):
    width = centres.shape[1]
    sums = prior_count * centres.astype(F32)
    mass = prior_count
    for state_ref in states:
        sums = sums + state_ref[:, :width]
        mass = mass + state_ref[:, width : width + 1]
    return sums / mass


def last_kernel(helpers, counts, share_rows, *refs):
    earlier, late, own = counts
    old, refs = refs[:1], refs[1:]
    given, refs = refs[: earlier + late], refs[earlier + late :]
    refined_ref, logs, refs = refs[0], refs[1 : 1 + own], refs[1 + own :]
    state_ref, ordered, share_ref, rows, old_ref, whole_ref, arrived, ready, kept = refs
    height = given[-1].shape[0]
    held = earlier * height
    centres = fetch([ref.at[height:] for ref in given[:helpers]], ordered, ready)
    given = [ref.at[:height] for ref in given]
    later = fetch(given[earlier:], rows.at[held:], arrived.at[earlier:])
    state = fetch(old, old_ref, kept)
    sooner = fetch(given[:earlier], rows, arrived)
    helper = lax.axis_index("hlp").astype(jnp.int32)
    settle(centres)
    centres = ordered[...]
    norms = square_norms(centres)
    turned = centres.T
    settle(later)
    accumulate(turned, norms, tiles_of(rows, held, rows.shape[0]), share_ref, state_ref, True)
    settle(state + sooner)
    states = (state_ref, old_ref)
    for turn in range(1, ITERS):
        centres = refine(centres, *states).astype(BF)
        states = (state_ref,)
        norms = square_norms(centres)
        turned = centres.T
        accumulate(turned, norms, tiles_of(rows, 0, rows.shape[0]), share_ref, state_ref, True)
    refined = refine(centres, *states)
    whole_ref[...] = refined[0:share_rows]
    written = fetch([whole_ref], refined_ref, kept)
    centres = refined.astype(BF)
    for j in range(helpers):
        place = pl.multiple_of(jnp.bitwise_xor(helper, j) * share_rows, share_rows)
        ordered[pl.ds(place, share_rows), :] = centres[j * share_rows : (j + 1) * share_rows]
    centres = ordered[...]
    norms = square_norms(centres)
    turned = centres.T
    own_rows = [rows[g * helpers * height : g * helpers * height + height, :] for g in range(own)]
    pair = 2 if 2 * height <= TILE and own % 2 == 0 else 1
    for g in range(0, own, pair):
        logits = energies(turned, norms, joined(own_rows[g : g + pair]))
        top = jnp.max(logits, axis=1, keepdims=True)
        total = jnp.log(jnp.sum(jnp.exp(logits - top), axis=1, keepdims=True))
        result = (logits - (top + total)).astype(BF)
        for i in range(pair):
            logs[g + i][...] = result[i * height : (i + 1) * height]
    settle(written)


def vmem(n):
    return [pl.BlockSpec(memory_space=pltpu.VMEM)] * n


HBM = pl.BlockSpec(memory_space=pltpu.HBM)
COST = pl.CostEstimate(flops=1, bytes_accessed=1, transcendentals=0)


def params(*arrays):
    held = sum(math.prod(a.shape) * a.dtype.itemsize for a in arrays)
    return pltpu.CompilerParams(vmem_limit_bytes=held + 8 * 1024 * 1024)


def in_hbm(value):
    return pltpu.with_memory_space_constraint(value, pltpu.HBM)


def after(value, *others):
    return lax.optimization_barrier((value,) + others)[0]


def hop(axis, size, step):
    pairs = [(i, i ^ step) for i in range(size)]
    return lambda x: lax.ppermute(x, axis, pairs)


def per_device(points, cluster_of, subcentroids):
    count, width = points.shape
    owners = lax.axis_size("own")
    helpers = lax.axis_size("hlp")
    depth = min(count // 2, 4 * count // owners)
    share_rows = subcentroids.shape[1]
    subs = share_rows * helpers
    groups = min(GROUPS, owners)
    per = owners // groups
    height = per * depth

    cluster = cluster_of.reshape(1, count)

    blocks = [jax.ShapeDtypeStruct((height + (0 if g else share_rows), width), BF) for g in range(groups)]
    packed = pl.pallas_call(
        functools.partial(pack_kernel, depth, owners),
        out_shape=blocks,
        in_specs=[HBM] * 3,
        out_specs=vmem(groups),
        scratch_shapes=[
            pltpu.VMEM(cluster.shape, jnp.int32),
            pltpu.VMEM(points.shape, BF),
            pltpu.SemaphoreType.DMA((3,)),
        ],
        compiler_params=params(points, *blocks),
        cost_estimate=COST,
        name="pack",
    )(in_hbm(cluster), in_hbm(points), in_hbm(subcentroids[0]))

    def across(block, g):
        if per == 1:
            return hop("own", owners, g)(block) if g else block
        done = []
        for j in range(per):
            step = g * per + j
            piece = block[j * depth : (j + 1) * depth]
            done.append(hop("own", owners, step)(piece) if step else piece)
        if block.shape[0] > height:
            done.append(block[height:])
        return joined(done)

    def over_chips(block):
        return [block] + [hop("hlp", helpers, step)(block) for step in range(2, helpers, 2)]

    def over_cores(held):
        return [x for block in held for x in (block, hop("hlp", helpers, 1)(block))]

    state = jax.ShapeDtypeStruct((subs, width + 128), F32)
    centre_table = jax.ShapeDtypeStruct((subs, width), BF)

    def scratch(n):
        return [
            state,
            centre_table,
            jax.ShapeDtypeStruct((n * height, subs), BF),
            jax.ShapeDtypeStruct((n * height, width), BF),
        ]

    def semaphores(*counts):
        return [pltpu.SemaphoreType.DMA((n,)) for n in counts]

    beside = hop("hlp", helpers, 1)
    moved = [packed[0]]
    for g in range(1, groups - 1):
        moved.append(across(packed[g], g))
    moved.append(across(after(packed[-1], moved[-1]) if groups > 1 else packed[-1], groups - 1))
    held = [over_chips(block) for block in moved]
    own_beside = beside(after(packed[0], held[0][1]))
    rows = [[moved[0], own_beside] + over_cores(held[0][1:])] + [over_cores(part) for part in held[1:-1]]
    given = [r for part in rows for r in part] + over_cores(held[-1][:1])
    own = scratch(len(given))
    sofar = pl.pallas_call(
        functools.partial(some_kernel, helpers, height),
        out_shape=state,
        in_specs=[HBM] * len(given),
        out_specs=HBM,
        scratch_shapes=[pltpu.VMEM(s.shape, s.dtype) for s in own] + semaphores(len(given), helpers, 1),
        compiler_params=params(*own),
        cost_estimate=COST,
        name="some_rows",
    )(*given)
    late = over_cores(held[-1][1:-1] + [after(held[-1][-1], sofar)])
    earlier = given
    logs = [jax.ShapeDtypeStruct((height, subs), BF)] * groups
    refined = jax.ShapeDtypeStruct((share_rows, width), F32)
    own = scratch(len(earlier) + len(late)) + [state, refined]
    refined, *logs = pl.pallas_call(
        functools.partial(last_kernel, helpers, (len(earlier), len(late), groups), share_rows),
        out_shape=[refined] + logs,
        in_specs=[HBM] * (1 + len(earlier) + len(late)),
        out_specs=[HBM] + vmem(groups),
        scratch_shapes=[pltpu.VMEM(s.shape, s.dtype) for s in own]
        + semaphores(len(earlier) + len(late), helpers, 1),
        compiler_params=params(*own, *logs),
        cost_estimate=COST,
        name="rounds",
    )(sofar, *[in_hbm(r) for r in earlier], *late)

    back = [across(logs[g], g) for g in reversed(range(groups))]
    places = jax.ShapeDtypeStruct((count, groups * height), BF)
    out = jax.ShapeDtypeStruct((count, subs), F32)
    where = pl.pallas_call(
        functools.partial(places_kernel, depth, owners),
        out_shape=places,
        in_specs=vmem(1),
        out_specs=pl.BlockSpec(memory_space=pltpu.VMEM),
        compiler_params=params(places),
        cost_estimate=COST,
        name="places",
    )(after(cluster, refined))
    log_resp = pl.pallas_call(
        unpack_kernel,
        out_shape=out,
        in_specs=vmem(1 + groups),
        out_specs=pl.BlockSpec(memory_space=pltpu.VMEM),
        compiler_params=params(places, *back, out),
        cost_estimate=COST,
        name="unpack",
    )(where, *back)
    return (refined[None], log_resp)


def solution(mesh):
    in_specs = (
        P(("grp", "own", "hlp"), None),
        P(("grp", "own", "hlp")),
        P(("grp", "own"), "hlp", None),
    )
    out_specs = (P(("grp", "own"), "hlp", None), P(("grp", "own", "hlp"), None))
    return jax.shard_map(
        per_device, mesh=mesh, in_specs=in_specs, out_specs=out_specs, check_vma=False
    )
```

```python
import functools
import math

import jax
import jax.numpy as jnp
from jax import lax
from jax.experimental import pallas as pl
from jax.experimental.pallas import tpu as pltpu
from jax.sharding import PartitionSpec as P

ITERS = 2
GROUPS = 4
TILE = 256

smoothing_factor = 16.0
prior_count = 1.0

EMPTY = 64.0
LIMIT = 32.0

BF = jnp.bfloat16
F32 = jnp.float32
TN = (((0,), (0,)), ((), ()))
NT = (((1,), (1,)), ((), ()))
NN = (((1,), (0,)), ((), ()))


def matmul(a, b, dims):
    return lax.dot_general(a, b, dims, preferred_element_type=F32)


def precedes(count):
    earlier = lax.broadcasted_iota(jnp.int32, (count, count), 0) < lax.broadcasted_iota(
        jnp.int32, (count, count), 1
    )
    return jnp.where(earlier, 1.0, 0.0).astype(BF)


def slots_of(cluster, earlier, depth, owners):
    count = cluster.shape[1]
    height = max(16, owners)
    offset = jnp.bitwise_xor(cluster, lax.axis_index("own").astype(jnp.int32))
    member = lax.broadcasted_iota(jnp.int32, (height, count), 0) == offset
    member = jnp.where(member, 1.0, 0.0)
    before = matmul(member.astype(BF), earlier, NN)
    rank = jnp.sum(before * member, axis=0, keepdims=True).astype(jnp.int32)
    return offset * depth + rank, jnp.sum(member, axis=1, keepdims=True)


def fetch(refs, target, arrived):
    height = refs[0].shape[0]
    copies = [
        pltpu.make_async_copy(ref, target.at[i * height : (i + 1) * height], arrived.at[i])
        for i, ref in enumerate(refs)
    ]
    for copy in copies:
        copy.start()
    return copies


def settle(copies):
    for copy in copies:
        copy.wait()


def pack_kernel(depth, owners, cluster_hbm, points_hbm, centres_hbm, *refs):
    *outs, cluster_ref, points_ref, arrived = refs
    names = pltpu.make_async_copy(cluster_hbm, cluster_ref, arrived.at[1])
    names.start()
    points = fetch([points_hbm], points_ref, arrived)
    height = outs[-1].shape[0]
    centres = fetch([centres_hbm], outs[0].at[height:], arrived.at[2:])
    earlier = precedes(cluster_ref.shape[1])
    names.wait()
    slot, tally = slots_of(cluster_ref[...], earlier, depth, owners)
    settle(points)
    points = points_ref[...]
    per = height // depth
    for g, out in enumerate(outs):
        rows = lax.broadcasted_iota(jnp.int32, (height, points.shape[0]), 0) + g * height
        pick = jnp.where(rows == slot, 1.0, 0.0).astype(BF)
        block = matmul(pick, points, NN)
        for j in range(per):
            held = tally[g * per + j : g * per + j + 1, :].astype(jnp.int32)
            local = lax.broadcasted_iota(jnp.int32, (depth, 1), 0)
            part = block[j * depth : (j + 1) * depth]
            out[j * depth : (j + 1) * depth, :] = jnp.where(local < held, part, EMPTY).astype(BF)
    settle(centres)


def places_kernel(depth, owners, cluster_ref, out):
    count, slots = out.shape
    slot, _ = slots_of(cluster_ref[...], precedes(count), depth, owners)
    column = jnp.broadcast_to(slot.astype(F32), (128, count)).T[:, 0:1].astype(jnp.int32)
    lanes = lax.broadcasted_iota(jnp.int32, (count, slots), 1)
    out[...] = jnp.where(lanes == column, 1.0, 0.0).astype(BF)


def unpack_kernel(places_ref, *refs):
    *logs, out = refs
    height = logs[0].shape[0]
    total = None
    for g, block in enumerate(logs[::-1]):
        term = matmul(places_ref[:, g * height : (g + 1) * height], block[...], NN)
        total = term if total is None else total + term
    out[...] = total


def square_norms(centres):
    wide = centres.astype(F32)
    column = jnp.sum(wide * wide, axis=1, keepdims=True)
    return jnp.broadcast_to(column, (column.shape[0], 128)).T[0:1]


def joined(parts):
    return parts[0] if len(parts) == 1 else jnp.concatenate(parts, axis=0)


def energies(centres, norms, rows):
    return matmul(rows, centres, NT) * (2.0 / smoothing_factor) - norms * (1.0 / smoothing_factor)


def accumulate(centres, norms, tiles, share_ref, state_ref, fresh):
    start = 0
    for rows in tiles:
        logits = energies(centres, norms, rows)
        top = jnp.max(logits, axis=1, keepdims=True)
        weight = jnp.exp(logits - top)
        live = jnp.where(rows[:, 0:1].astype(F32) < LIMIT, 1.0, 0.0)
        scale = live / jnp.sum(weight, axis=1, keepdims=True)
        share_ref[start : start + rows.shape[0], :] = (weight * scale).astype(BF)
        start += rows.shape[0]
    subs, width = centres.shape
    start = 0
    for i, rows in enumerate(tiles):
        share = share_ref[start : start + rows.shape[0], :]
        mass = matmul(share, jnp.ones((rows.shape[0], 128), BF), TN)
        part = matmul(share, rows, TN)
        if fresh and i == 0:
            state_ref[:subs, width:] = mass
            state_ref[:subs, :width] = part
        else:
            state_ref[:subs, width:] += mass
            state_ref[:subs, :width] += part
        start += rows.shape[0]


def tiles_of(rows, first, last):
    return [rows[r : r + TILE, :] for r in range(first, last, TILE)]


def some_kernel(helpers, height, *refs):
    *given, out, state_ref, centres_ref, share_ref, rows, arrived, ready, kept = refs
    centres = fetch([ref.at[height:] for ref in given[:helpers]], centres_ref, ready)
    copies = fetch([ref.at[:height] for ref in given], rows, arrived)
    settle(centres)
    centres = centres_ref[...]
    norms = square_norms(centres)
    settle(copies)
    accumulate(centres, norms, tiles_of(rows, 0, rows.shape[0]), share_ref, state_ref, True)
    subs = centres.shape[0]
    state_ref[subs:, :subs] = jnp.broadcast_to(norms, (8, subs))
    settle(fetch([state_ref], out, kept))


def refine(centres, *states):
    subs, width = centres.shape
    sums = prior_count * centres.astype(F32)
    mass = prior_count
    for state_ref in states:
        sums = sums + state_ref[:subs, :width]
        mass = mass + state_ref[:subs, width : width + 1]
    return sums / mass


def last_kernel(helpers, counts, share_rows, *refs):
    earlier, late, own = counts
    old, refs = refs[:1], refs[1:]
    given, refs = refs[: earlier + late], refs[earlier + late :]
    refined_ref, logs, refs = refs[0], refs[1 : 1 + own], refs[1 + own :]
    state_ref, ordered, share_ref, rows, old_ref, whole_ref, arrived, ready, kept = refs
    height = given[-1].shape[0]
    held = earlier * height
    centres = fetch([ref.at[height:] for ref in given[:helpers]], ordered, ready)
    given = [ref.at[:height] for ref in given]
    later = fetch(given[earlier:], rows.at[held:], arrived.at[earlier:])
    state = fetch(old, old_ref, kept)
    sooner = fetch(given[:earlier], rows, arrived)
    helper = lax.axis_index("hlp").astype(jnp.int32)
    settle(centres + state + later)
    centres = ordered[...]
    norms = old_ref[centres.shape[0] : centres.shape[0] + 1, : centres.shape[0]]
    accumulate(centres, norms, tiles_of(rows, held, rows.shape[0]), share_ref, state_ref, True)
    settle(sooner)
    states = (state_ref, old_ref)
    for turn in range(1, ITERS):
        centres = refine(centres, *states).astype(BF)
        states = (state_ref,)
        norms = square_norms(centres)
        accumulate(centres, norms, tiles_of(rows, 0, rows.shape[0]), share_ref, state_ref, True)
    refined = refine(centres, *states)
    whole_ref[...] = refined[0:share_rows]
    written = fetch([whole_ref], refined_ref, kept)
    centres = refined.astype(BF)
    for j in range(helpers):
        place = pl.multiple_of(jnp.bitwise_xor(helper, j) * share_rows, share_rows)
        ordered[pl.ds(place, share_rows), :] = centres[j * share_rows : (j + 1) * share_rows]
    centres = ordered[...]
    norms = square_norms(centres)
    own_rows = [rows[g * helpers * height : g * helpers * height + height, :] for g in range(own)]
    pair = 2 if 2 * height <= TILE and own % 2 == 0 else 1
    for g in range(0, own, pair):
        logits = energies(centres, norms, joined(own_rows[g : g + pair]))
        top = jnp.max(logits, axis=1, keepdims=True)
        total = jnp.log(jnp.sum(jnp.exp(logits - top), axis=1, keepdims=True))
        result = (logits - (top + total)).astype(BF)
        for i in range(pair):
            logs[g + i][...] = result[i * height : (i + 1) * height]
    settle(written)


def vmem(n):
    return [pl.BlockSpec(memory_space=pltpu.VMEM)] * n


HBM = pl.BlockSpec(memory_space=pltpu.HBM)
COST = pl.CostEstimate(flops=1, bytes_accessed=1, transcendentals=0)


def params(*arrays):
    held = sum(math.prod(a.shape) * a.dtype.itemsize for a in arrays)
    return pltpu.CompilerParams(vmem_limit_bytes=held + 8 * 1024 * 1024)


def in_hbm(value):
    return pltpu.with_memory_space_constraint(value, pltpu.HBM)


def after(value, *others):
    return lax.optimization_barrier((value,) + others)[0]


def hop(axis, size, step):
    pairs = [(i, i ^ step) for i in range(size)]
    return lambda x: lax.ppermute(x, axis, pairs)


def per_device(points, cluster_of, subcentroids):
    count, width = points.shape
    owners = lax.axis_size("own")
    helpers = lax.axis_size("hlp")
    depth = min(count // 2, 4 * count // owners)
    share_rows = subcentroids.shape[1]
    subs = share_rows * helpers
    groups = min(GROUPS, owners)
    per = owners // groups
    height = per * depth

    cluster = cluster_of.reshape(1, count)

    blocks = [jax.ShapeDtypeStruct((height + (0 if g else share_rows), width), BF) for g in range(groups)]
    packed = pl.pallas_call(
        functools.partial(pack_kernel, depth, owners),
        out_shape=blocks,
        in_specs=[HBM] * 3,
        out_specs=vmem(groups),
        scratch_shapes=[
            pltpu.VMEM(cluster.shape, jnp.int32),
            pltpu.VMEM(points.shape, BF),
            pltpu.SemaphoreType.DMA((3,)),
        ],
        compiler_params=params(points, *blocks),
        cost_estimate=COST,
        name="pack",
    )(in_hbm(cluster), in_hbm(points), in_hbm(subcentroids[0]))

    def across(block, g):
        if per == 1:
            return hop("own", owners, g)(block) if g else block
        done = []
        for j in range(per):
            step = g * per + j
            piece = block[j * depth : (j + 1) * depth]
            done.append(hop("own", owners, step)(piece) if step else piece)
        if block.shape[0] > height:
            done.append(block[height:])
        return joined(done)

    def over_chips(block):
        return [block] + [hop("hlp", helpers, step)(block) for step in range(2, helpers, 2)]

    def over_cores(held):
        return [x for block in held for x in (block, hop("hlp", helpers, 1)(block))]

    state = jax.ShapeDtypeStruct((subs + 8, width + 128), F32)
    centre_table = jax.ShapeDtypeStruct((subs, width), BF)

    def scratch(n):
        return [
            state,
            centre_table,
            jax.ShapeDtypeStruct((n * height, subs), BF),
            jax.ShapeDtypeStruct((n * height, width), BF),
        ]

    def semaphores(*counts):
        return [pltpu.SemaphoreType.DMA((n,)) for n in counts]

    beside = hop("hlp", helpers, 1)
    moved = [across(packed[0], 0)]
    for g in range(1, groups - 1):
        moved.append(across(packed[g], g))
    moved.append(across(after(packed[-1], moved[-1]) if groups > 1 else packed[-1], groups - 1))
    held = [over_chips(block) for block in moved]
    own_beside = beside(after(moved[0], held[0][1]))
    rows = [[moved[0], own_beside] + over_cores(held[0][1:])] + [over_cores(part) for part in held[1:-1]]
    given = [r for part in rows for r in part] + over_cores(held[-1][:1])
    own = scratch(len(given))
    sofar = pl.pallas_call(
        functools.partial(some_kernel, helpers, height),
        out_shape=state,
        in_specs=[HBM] * len(given),
        out_specs=HBM,
        scratch_shapes=[pltpu.VMEM(s.shape, s.dtype) for s in own] + semaphores(len(given), helpers, 1),
        compiler_params=params(*own),
        cost_estimate=COST,
        name="some_rows",
    )(*given)
    late = over_cores(held[-1][1:-1] + [after(held[-1][-1], sofar)])
    earlier = given
    logs = [jax.ShapeDtypeStruct((height, subs), BF)] * groups
    refined = jax.ShapeDtypeStruct((share_rows, width), F32)
    own = scratch(len(earlier) + len(late)) + [state, refined]
    refined, *logs = pl.pallas_call(
        functools.partial(last_kernel, helpers, (len(earlier), len(late), groups), share_rows),
        out_shape=[refined] + logs,
        in_specs=[HBM] * (1 + len(earlier) + len(late)),
        out_specs=[HBM] + vmem(groups),
        scratch_shapes=[pltpu.VMEM(s.shape, s.dtype) for s in own]
        + semaphores(len(earlier) + len(late), helpers, 1),
        compiler_params=params(*own, *logs),
        cost_estimate=COST,
        name="rounds",
    )(sofar, *[in_hbm(r) for r in earlier], *late)

    back = [across(logs[g], g) for g in reversed(range(groups))]
    places = jax.ShapeDtypeStruct((count, groups * height), BF)
    out = jax.ShapeDtypeStruct((count, subs), F32)
    where = pl.pallas_call(
        functools.partial(places_kernel, depth, owners),
        out_shape=places,
        in_specs=vmem(1),
        out_specs=pl.BlockSpec(memory_space=pltpu.VMEM),
        compiler_params=params(places),
        cost_estimate=COST,
        name="places",
    )(after(cluster, refined))
    log_resp = pl.pallas_call(
        unpack_kernel,
        out_shape=out,
        in_specs=vmem(1 + groups),
        out_specs=pl.BlockSpec(memory_space=pltpu.VMEM),
        compiler_params=params(places, *back, out),
        cost_estimate=COST,
        name="unpack",
    )(where, *back)
    return (refined[None], log_resp)


def solution(mesh):
    in_specs = (
        P(("grp", "own", "hlp"), None),
        P(("grp", "own", "hlp")),
        P(("grp", "own"), "hlp", None),
    )
    out_specs = (P(("grp", "own"), "hlp", None), P(("grp", "own", "hlp"), None))
    return jax.shard_map(
        per_device, mesh=mesh, in_specs=in_specs, out_specs=out_specs, check_vma=False
    )
```

```python
import functools
import math

import jax
import jax.numpy as jnp
from jax import lax
from jax.experimental import pallas as pl
from jax.experimental.pallas import tpu as pltpu
from jax.sharding import PartitionSpec as P

ITERS = 2
GROUPS = 4
TILE = 256

smoothing_factor = 16.0
prior_count = 1.0

EMPTY = 64.0
LIMIT = 32.0

BF = jnp.bfloat16
F32 = jnp.float32
TN = (((0,), (0,)), ((), ()))
NT = (((1,), (1,)), ((), ()))
NN = (((1,), (0,)), ((), ()))


def matmul(a, b, dims):
    return lax.dot_general(a, b, dims, preferred_element_type=F32)


def precedes(count):
    earlier = lax.broadcasted_iota(jnp.int32, (count, count), 0) < lax.broadcasted_iota(
        jnp.int32, (count, count), 1
    )
    return jnp.where(earlier, 1.0, 0.0).astype(BF)


def slots_of(cluster, earlier, depth, owners):
    count = cluster.shape[1]
    height = max(16, owners)
    offset = jnp.bitwise_xor(cluster, lax.axis_index("own").astype(jnp.int32))
    member = lax.broadcasted_iota(jnp.int32, (height, count), 0) == offset
    member = jnp.where(member, 1.0, 0.0)
    before = matmul(member.astype(BF), earlier, NN)
    rank = jnp.sum(before * member, axis=0, keepdims=True).astype(jnp.int32)
    return offset * depth + rank, jnp.sum(member, axis=1, keepdims=True)


def fetch(refs, target, arrived):
    height = refs[0].shape[0]
    copies = [
        pltpu.make_async_copy(ref, target.at[i * height : (i + 1) * height], arrived.at[i])
        for i, ref in enumerate(refs)
    ]
    for copy in copies:
        copy.start()
    return copies


def settle(copies):
    for copy in copies:
        copy.wait()


def pack_kernel(depth, owners, cluster_hbm, points_hbm, centres_hbm, *refs):
    *outs, cluster_ref, points_ref, arrived = refs
    names = pltpu.make_async_copy(cluster_hbm, cluster_ref, arrived.at[1])
    names.start()
    points = fetch([points_hbm], points_ref, arrived)
    height = outs[-1].shape[0]
    centres = fetch([centres_hbm], outs[0].at[height:], arrived.at[2:])
    earlier = precedes(cluster_ref.shape[1])
    names.wait()
    slot, tally = slots_of(cluster_ref[...], earlier, depth, owners)
    settle(points)
    points = points_ref[...]
    per = height // depth
    for g, out in enumerate(outs):
        rows = lax.broadcasted_iota(jnp.int32, (height, points.shape[0]), 0) + g * height
        pick = jnp.where(rows == slot, 1.0, 0.0).astype(BF)
        block = matmul(pick, points, NN)
        for j in range(per):
            held = tally[g * per + j : g * per + j + 1, :].astype(jnp.int32)
            local = lax.broadcasted_iota(jnp.int32, (depth, 1), 0)
            part = block[j * depth : (j + 1) * depth]
            out[j * depth : (j + 1) * depth, :] = jnp.where(local < held, part, EMPTY).astype(BF)
    settle(centres)


def places_kernel(depth, owners, cluster_ref, out):
    count, slots = out.shape
    slot, _ = slots_of(cluster_ref[...], precedes(count), depth, owners)
    column = jnp.broadcast_to(slot.astype(F32), (128, count)).T[:, 0:1].astype(jnp.int32)
    lanes = lax.broadcasted_iota(jnp.int32, (count, slots), 1)
    out[...] = jnp.where(lanes == column, 1.0, 0.0).astype(BF)


def unpack_kernel(places_ref, *refs):
    *logs, out = refs
    height = logs[0].shape[0]
    total = None
    for g, block in enumerate(logs[::-1]):
        term = matmul(places_ref[:, g * height : (g + 1) * height], block[...], NN)
        total = term if total is None else total + term
    out[...] = total


def square_norms(centres):
    wide = centres.astype(F32)
    column = jnp.sum(wide * wide, axis=1, keepdims=True)
    return jnp.broadcast_to(column, (column.shape[0], 128)).T[0:1]


def joined(parts):
    return parts[0] if len(parts) == 1 else jnp.concatenate(parts, axis=0)


def energies(centres, norms, rows):
    return matmul(rows, centres, NT) * (2.0 / smoothing_factor) - norms * (1.0 / smoothing_factor)


def accumulate(centres, norms, tiles, share_ref, state_ref, fresh):
    start = 0
    for rows in tiles:
        logits = energies(centres, norms, rows)
        top = jnp.max(logits, axis=1, keepdims=True)
        weight = jnp.exp(logits - top)
        live = jnp.where(rows[:, 0:1].astype(F32) < LIMIT, 1.0, 0.0)
        scale = live / jnp.sum(weight, axis=1, keepdims=True)
        share_ref[start : start + rows.shape[0], :] = (weight * scale).astype(BF)
        start += rows.shape[0]
    subs, width = centres.shape
    start = 0
    for i, rows in enumerate(tiles):
        share = share_ref[start : start + rows.shape[0], :]
        mass = matmul(share, jnp.ones((rows.shape[0], 128), BF), TN)
        part = matmul(share, rows, TN)
        if fresh and i == 0:
            state_ref[:subs, width:] = mass
            state_ref[:subs, :width] = part
        else:
            state_ref[:subs, width:] += mass
            state_ref[:subs, :width] += part
        start += rows.shape[0]


def tiles_of(rows, first, last):
    return [rows[r : r + TILE, :] for r in range(first, last, TILE)]


def some_kernel(helpers, height, *refs):
    *given, out, state_ref, centres_ref, share_ref, rows, arrived, ready, kept = refs
    centres = fetch([ref.at[height:] for ref in given[:helpers]], centres_ref, ready)
    copies = fetch([ref.at[:height] for ref in given], rows, arrived)
    settle(centres)
    centres = centres_ref[...]
    norms = square_norms(centres)
    settle(copies)
    accumulate(centres, norms, tiles_of(rows, 0, rows.shape[0]), share_ref, state_ref, True)
    subs = centres.shape[0]
    state_ref[subs:, :subs] = jnp.broadcast_to(norms, (8, subs))
    settle(fetch([state_ref], out, kept))


def refine(centres, *states):
    subs, width = centres.shape
    sums = prior_count * centres.astype(F32)
    mass = prior_count
    for state_ref in states:
        sums = sums + state_ref[:subs, :width]
        mass = mass + state_ref[:subs, width : width + 1]
    return sums / mass


def last_kernel(helpers, counts, share_rows, *refs):
    earlier, late, own = counts
    old, refs = refs[:1], refs[1:]
    given, refs = refs[: earlier + late], refs[earlier + late :]
    refined_ref, logs, refs = refs[0], refs[1 : 1 + own], refs[1 + own :]
    state_ref, ordered, share_ref, rows, old_ref, whole_ref, arrived, ready, kept = refs
    height = given[-1].shape[0]
    held = earlier * height
    subs = helpers * share_rows
    centres = fetch([ref.at[height:] for ref in given[:helpers]], ordered, ready)
    given = [ref.at[:height] for ref in given]
    norms = fetch([old[0].at[subs:]], old_ref.at[subs:], kept.at[1:])
    later = fetch(given[earlier:], rows.at[held:], arrived.at[earlier:])
    state = fetch([old[0].at[:subs]], old_ref.at[:subs], kept)
    sooner = fetch(given[:earlier], rows, arrived)
    helper = lax.axis_index("hlp").astype(jnp.int32)
    settle(centres + norms + later)
    centres = ordered[...]
    norms = old_ref[subs : subs + 1, :subs]
    accumulate(centres, norms, tiles_of(rows, held, rows.shape[0]), share_ref, state_ref, True)
    settle(state + sooner)
    states = (state_ref, old_ref)
    for turn in range(1, ITERS):
        centres = refine(centres, *states).astype(BF)
        states = (state_ref,)
        norms = square_norms(centres)
        accumulate(centres, norms, tiles_of(rows, 0, rows.shape[0]), share_ref, state_ref, True)
    refined = refine(centres, *states)
    whole_ref[...] = refined[0:share_rows]
    written = fetch([whole_ref], refined_ref, kept)
    centres = refined.astype(BF)
    for j in range(helpers):
        place = pl.multiple_of(jnp.bitwise_xor(helper, j) * share_rows, share_rows)
        ordered[pl.ds(place, share_rows), :] = centres[j * share_rows : (j + 1) * share_rows]
    centres = ordered[...]
    norms = square_norms(centres)
    own_rows = [rows[g * helpers * height : g * helpers * height + height, :] for g in range(own)]
    pair = 2 if 2 * height <= TILE and own % 2 == 0 else 1
    for g in range(0, own, pair):
        logits = energies(centres, norms, joined(own_rows[g : g + pair]))
        top = jnp.max(logits, axis=1, keepdims=True)
        total = jnp.log(jnp.sum(jnp.exp(logits - top), axis=1, keepdims=True))
        result = (logits - (top + total)).astype(BF)
        for i in range(pair):
            logs[g + i][...] = result[i * height : (i + 1) * height]
    settle(written)


def vmem(n):
    return [pl.BlockSpec(memory_space=pltpu.VMEM)] * n


HBM = pl.BlockSpec(memory_space=pltpu.HBM)
COST = pl.CostEstimate(flops=1, bytes_accessed=1, transcendentals=0)


def params(*arrays):
    held = sum(math.prod(a.shape) * a.dtype.itemsize for a in arrays)
    return pltpu.CompilerParams(vmem_limit_bytes=held + 8 * 1024 * 1024)


def in_hbm(value):
    return pltpu.with_memory_space_constraint(value, pltpu.HBM)


def after(value, *others):
    return lax.optimization_barrier((value,) + others)[0]


def hop(axis, size, step):
    pairs = [(i, i ^ step) for i in range(size)]
    return lambda x: lax.ppermute(x, axis, pairs)


def per_device(points, cluster_of, subcentroids):
    count, width = points.shape
    owners = lax.axis_size("own")
    helpers = lax.axis_size("hlp")
    depth = min(count // 2, 4 * count // owners)
    share_rows = subcentroids.shape[1]
    subs = share_rows * helpers
    groups = min(GROUPS, owners)
    per = owners // groups
    height = per * depth

    cluster = cluster_of.reshape(1, count)

    blocks = [jax.ShapeDtypeStruct((height + (0 if g else share_rows), width), BF) for g in range(groups)]
    packed = pl.pallas_call(
        functools.partial(pack_kernel, depth, owners),
        out_shape=blocks,
        in_specs=[HBM] * 3,
        out_specs=vmem(groups),
        scratch_shapes=[
            pltpu.VMEM(cluster.shape, jnp.int32),
            pltpu.VMEM(points.shape, BF),
            pltpu.SemaphoreType.DMA((3,)),
        ],
        compiler_params=params(points, *blocks),
        cost_estimate=COST,
        name="pack",
    )(in_hbm(cluster), in_hbm(points), in_hbm(subcentroids[0]))

    def across(block, g):
        if per == 1:
            return hop("own", owners, g)(block) if g else block
        done = []
        for j in range(per):
            step = g * per + j
            piece = block[j * depth : (j + 1) * depth]
            done.append(hop("own", owners, step)(piece) if step else piece)
        if block.shape[0] > height:
            done.append(block[height:])
        return joined(done)

    def over_chips(block):
        return [block] + [hop("hlp", helpers, step)(block) for step in range(2, helpers, 2)]

    def over_cores(held):
        return [x for block in held for x in (block, hop("hlp", helpers, 1)(block))]

    state = jax.ShapeDtypeStruct((subs + 8, width + 128), F32)
    centre_table = jax.ShapeDtypeStruct((subs, width), BF)

    def scratch(n):
        return [
            state,
            centre_table,
            jax.ShapeDtypeStruct((n * height, subs), BF),
            jax.ShapeDtypeStruct((n * height, width), BF),
        ]

    def semaphores(*counts):
        return [pltpu.SemaphoreType.DMA((n,)) for n in counts]

    beside = hop("hlp", helpers, 1)
    moved = [across(packed[0], 0)]
    for g in range(1, groups - 1):
        moved.append(across(packed[g], g))
    moved.append(across(after(packed[-1], moved[-1]) if groups > 1 else packed[-1], groups - 1))
    held = [over_chips(block) for block in moved]
    own_beside = beside(after(moved[0], held[0][1]))
    rows = [[moved[0], own_beside] + over_cores(held[0][1:])] + [over_cores(part) for part in held[1:-1]]
    given = [r for part in rows for r in part] + over_cores(held[-1][:1])
    own = scratch(len(given))
    sofar = pl.pallas_call(
        functools.partial(some_kernel, helpers, height),
        out_shape=state,
        in_specs=[HBM] * len(given),
        out_specs=HBM,
        scratch_shapes=[pltpu.VMEM(s.shape, s.dtype) for s in own] + semaphores(len(given), helpers, 1),
        compiler_params=params(*own),
        cost_estimate=COST,
        name="some_rows",
    )(*given)
    late = over_cores(held[-1][1:-1] + [after(held[-1][-1], sofar)])
    earlier = given
    logs = [jax.ShapeDtypeStruct((height, subs), BF)] * groups
    refined = jax.ShapeDtypeStruct((share_rows, width), F32)
    own = scratch(len(earlier) + len(late)) + [state, refined]
    refined, *logs = pl.pallas_call(
        functools.partial(last_kernel, helpers, (len(earlier), len(late), groups), share_rows),
        out_shape=[refined] + logs,
        in_specs=[HBM] * (1 + len(earlier) + len(late)),
        out_specs=[HBM] + vmem(groups),
        scratch_shapes=[pltpu.VMEM(s.shape, s.dtype) for s in own]
        + semaphores(len(earlier) + len(late), helpers, 2),
        compiler_params=params(*own, *logs),
        cost_estimate=COST,
        name="rounds",
    )(sofar, *[in_hbm(r) for r in earlier[: 3 * helpers - 2]], *earlier[3 * helpers - 2 :], *late)

    back = [across(logs[g], g) for g in reversed(range(groups))]
    places = jax.ShapeDtypeStruct((count, groups * height), BF)
    out = jax.ShapeDtypeStruct((count, subs), F32)
    where = pl.pallas_call(
        functools.partial(places_kernel, depth, owners),
        out_shape=places,
        in_specs=vmem(1),
        out_specs=pl.BlockSpec(memory_space=pltpu.VMEM),
        compiler_params=params(places),
        cost_estimate=COST,
        name="places",
    )(after(cluster, refined))
    log_resp = pl.pallas_call(
        unpack_kernel,
        out_shape=out,
        in_specs=vmem(1 + groups),
        out_specs=pl.BlockSpec(memory_space=pltpu.VMEM),
        compiler_params=params(places, *back, out),
        cost_estimate=COST,
        name="unpack",
    )(where, *back)
    return (refined[None], log_resp)


def solution(mesh):
    in_specs = (
        P(("grp", "own", "hlp"), None),
        P(("grp", "own", "hlp")),
        P(("grp", "own"), "hlp", None),
    )
    out_specs = (P(("grp", "own"), "hlp", None), P(("grp", "own", "hlp"), None))
    return jax.shard_map(
        per_device, mesh=mesh, in_specs=in_specs, out_specs=out_specs, check_vma=False
    )
```

```python
import functools
import math

import jax
import jax.numpy as jnp
from jax import lax
from jax.experimental import pallas as pl
from jax.experimental.pallas import tpu as pltpu
from jax.sharding import PartitionSpec as P

ITERS = 2
GROUPS = 4
TILE = 256

smoothing_factor = 16.0
prior_count = 1.0

EMPTY = 64.0
LIMIT = 32.0

BF = jnp.bfloat16
F32 = jnp.float32
TN = (((0,), (0,)), ((), ()))
NT = (((1,), (1,)), ((), ()))
NN = (((1,), (0,)), ((), ()))


def matmul(a, b, dims):
    return lax.dot_general(a, b, dims, preferred_element_type=F32)


def precedes(count):
    earlier = lax.broadcasted_iota(jnp.int32, (count, count), 0) < lax.broadcasted_iota(
        jnp.int32, (count, count), 1
    )
    return jnp.where(earlier, 1.0, 0.0).astype(BF)


def slots_of(cluster, earlier, depth, owners):
    count = cluster.shape[1]
    height = max(16, owners)
    offset = jnp.bitwise_xor(cluster, lax.axis_index("own").astype(jnp.int32))
    member = lax.broadcasted_iota(jnp.int32, (height, count), 0) == offset
    member = jnp.where(member, 1.0, 0.0)
    before = matmul(member.astype(BF), earlier, NN)
    rank = jnp.sum(before * member, axis=0, keepdims=True).astype(jnp.int32)
    return offset * depth + rank, jnp.sum(member, axis=1, keepdims=True)


def fetch(refs, target, arrived):
    height = refs[0].shape[0]
    copies = [
        pltpu.make_async_copy(ref, target.at[i * height : (i + 1) * height], arrived.at[i])
        for i, ref in enumerate(refs)
    ]
    for copy in copies:
        copy.start()
    return copies


def settle(copies):
    for copy in copies:
        copy.wait()


def pack_kernel(depth, owners, cluster_hbm, points_hbm, centres_hbm, *refs):
    *outs, cluster_ref, points_ref, arrived = refs
    names = pltpu.make_async_copy(cluster_hbm, cluster_ref, arrived.at[1])
    names.start()
    points = fetch([points_hbm], points_ref, arrived)
    height = outs[-1].shape[0]
    centres = fetch([centres_hbm], outs[0].at[height:], arrived.at[2:])
    earlier = precedes(cluster_ref.shape[1])
    names.wait()
    slot, tally = slots_of(cluster_ref[...], earlier, depth, owners)
    settle(points)
    points = points_ref[...]
    per = height // depth
    for g, out in enumerate(outs):
        rows = lax.broadcasted_iota(jnp.int32, (height, points.shape[0]), 0) + g * height
        pick = jnp.where(rows == slot, 1.0, 0.0).astype(BF)
        block = matmul(pick, points, NN)
        for j in range(per):
            held = tally[g * per + j : g * per + j + 1, :].astype(jnp.int32)
            local = lax.broadcasted_iota(jnp.int32, (depth, 1), 0)
            part = block[j * depth : (j + 1) * depth]
            out[j * depth : (j + 1) * depth, :] = jnp.where(local < held, part, EMPTY).astype(BF)
    settle(centres)


def places_kernel(depth, owners, cluster_ref, out):
    count, slots = out.shape
    slot, _ = slots_of(cluster_ref[...], precedes(count), depth, owners)
    column = jnp.broadcast_to(slot.astype(F32), (128, count)).T[:, 0:1].astype(jnp.int32)
    lanes = lax.broadcasted_iota(jnp.int32, (count, slots), 1)
    out[...] = jnp.where(lanes == column, 1.0, 0.0).astype(BF)


def leaving(groups):
    return [groups - 1, *range(1, groups - 1), 0]


def unpack_kernel(places_ref, *refs):
    *logs, out = refs
    height = logs[0].shape[0]
    total = None
    for g, block in zip(leaving(len(logs)), logs):
        term = matmul(places_ref[:, g * height : (g + 1) * height], block[...], NN)
        total = term if total is None else total + term
    out[...] = total


def square_norms(centres):
    wide = centres.astype(F32)
    column = jnp.sum(wide * wide, axis=1, keepdims=True)
    return jnp.broadcast_to(column, (column.shape[0], 128)).T[0:1]


def joined(parts):
    return parts[0] if len(parts) == 1 else jnp.concatenate(parts, axis=0)


def energies(centres, norms, rows):
    return matmul(rows, centres, NT) * (2.0 / smoothing_factor) - norms * (1.0 / smoothing_factor)


def accumulate(centres, norms, tiles, share_ref, state_ref, fresh):
    start = 0
    for rows in tiles:
        logits = energies(centres, norms, rows)
        top = jnp.max(logits, axis=1, keepdims=True)
        weight = jnp.exp(logits - top)
        live = jnp.where(rows[:, 0:1].astype(F32) < LIMIT, 1.0, 0.0)
        scale = live / jnp.sum(weight, axis=1, keepdims=True)
        share_ref[start : start + rows.shape[0], :] = (weight * scale).astype(BF)
        start += rows.shape[0]
    subs, width = centres.shape
    start = 0
    for i, rows in enumerate(tiles):
        share = share_ref[start : start + rows.shape[0], :]
        mass = matmul(share, jnp.ones((rows.shape[0], 128), BF), TN)
        part = matmul(share, rows, TN)
        if fresh and i == 0:
            state_ref[:subs, width:] = mass
            state_ref[:subs, :width] = part
        else:
            state_ref[:subs, width:] += mass
            state_ref[:subs, :width] += part
        start += rows.shape[0]


def tiles_of(rows, first, last):
    return [rows[r : r + TILE, :] for r in range(first, last, TILE)]


def some_kernel(helpers, height, *refs):
    *given, out, state_ref, centres_ref, share_ref, rows, arrived, ready, kept = refs
    centres = fetch([ref.at[height:] for ref in given[:helpers]], centres_ref, ready)
    copies = fetch([ref.at[:height] for ref in given], rows, arrived)
    settle(centres)
    centres = centres_ref[...]
    norms = square_norms(centres)
    settle(copies)
    accumulate(centres, norms, tiles_of(rows, 0, rows.shape[0]), share_ref, state_ref, True)
    subs = centres.shape[0]
    state_ref[subs:, :subs] = jnp.broadcast_to(norms, (8, subs))
    settle(fetch([state_ref], out, kept))


def refine(centres, *states):
    subs, width = centres.shape
    sums = prior_count * centres.astype(F32)
    mass = prior_count
    for state_ref in states:
        sums = sums + state_ref[:subs, :width]
        mass = mass + state_ref[:subs, width : width + 1]
    return sums / mass


def last_kernel(helpers, counts, share_rows, *refs):
    earlier, late, own = counts
    old, refs = refs[:1], refs[1:]
    given, refs = refs[: earlier + late], refs[earlier + late :]
    refined_ref, logs, refs = refs[0], refs[1 : 1 + own], refs[1 + own :]
    state_ref, ordered, share_ref, rows, old_ref, whole_ref, arrived, ready, kept = refs
    height = given[-1].shape[0]
    held = earlier * height
    subs = helpers * share_rows
    centres = fetch([ref.at[height:] for ref in given[:helpers]], ordered, ready)
    given = [ref.at[:height] for ref in given]
    norms = fetch([old[0].at[subs:]], old_ref.at[subs:], kept.at[1:])
    later = fetch(given[earlier:], rows.at[held:], arrived.at[earlier:])
    state = fetch([old[0].at[:subs]], old_ref.at[:subs], kept)
    sooner = fetch(given[:earlier], rows, arrived)
    helper = lax.axis_index("hlp").astype(jnp.int32)
    settle(centres + norms + later)
    centres = ordered[...]
    norms = old_ref[subs : subs + 1, :subs]
    accumulate(centres, norms, tiles_of(rows, held, rows.shape[0]), share_ref, state_ref, True)
    settle(state + sooner)
    states = (state_ref, old_ref)
    for turn in range(1, ITERS):
        centres = refine(centres, *states).astype(BF)
        states = (state_ref,)
        norms = square_norms(centres)
        accumulate(centres, norms, tiles_of(rows, 0, rows.shape[0]), share_ref, state_ref, True)
    refined = refine(centres, *states)
    whole_ref[...] = refined[0:share_rows]
    written = fetch([whole_ref], refined_ref, kept)
    centres = refined.astype(BF)
    for j in range(helpers):
        place = pl.multiple_of(jnp.bitwise_xor(helper, j) * share_rows, share_rows)
        ordered[pl.ds(place, share_rows), :] = centres[j * share_rows : (j + 1) * share_rows]
    centres = ordered[...]
    norms = square_norms(centres)
    own_rows = [rows[g * helpers * height : g * helpers * height + height, :] for g in range(own)]
    pair = 2 if 2 * height <= TILE and own % 2 == 0 else 1
    for g in range(0, own, pair):
        logits = energies(centres, norms, joined(own_rows[g : g + pair]))
        top = jnp.max(logits, axis=1, keepdims=True)
        total = jnp.log(jnp.sum(jnp.exp(logits - top), axis=1, keepdims=True))
        result = (logits - (top + total)).astype(BF)
        for i in range(pair):
            logs[g + i][...] = result[i * height : (i + 1) * height]
    settle(written)


def vmem(n):
    return [pl.BlockSpec(memory_space=pltpu.VMEM)] * n


HBM = pl.BlockSpec(memory_space=pltpu.HBM)
COST = pl.CostEstimate(flops=1, bytes_accessed=1, transcendentals=0)


def params(*arrays):
    held = sum(math.prod(a.shape) * a.dtype.itemsize for a in arrays)
    return pltpu.CompilerParams(vmem_limit_bytes=held + 8 * 1024 * 1024)


def in_hbm(value):
    return pltpu.with_memory_space_constraint(value, pltpu.HBM)


def after(value, *others):
    return lax.optimization_barrier((value,) + others)[0]


def hop(axis, size, step):
    pairs = [(i, i ^ step) for i in range(size)]
    return lambda x: lax.ppermute(x, axis, pairs)


def per_device(points, cluster_of, subcentroids):
    count, width = points.shape
    owners = lax.axis_size("own")
    helpers = lax.axis_size("hlp")
    depth = min(count // 2, 4 * count // owners)
    share_rows = subcentroids.shape[1]
    subs = share_rows * helpers
    groups = min(GROUPS, owners)
    per = owners // groups
    height = per * depth

    cluster = cluster_of.reshape(1, count)

    blocks = [jax.ShapeDtypeStruct((height + (0 if g else share_rows), width), BF) for g in range(groups)]
    packed = pl.pallas_call(
        functools.partial(pack_kernel, depth, owners),
        out_shape=blocks,
        in_specs=[HBM] * 3,
        out_specs=vmem(groups),
        scratch_shapes=[
            pltpu.VMEM(cluster.shape, jnp.int32),
            pltpu.VMEM(points.shape, BF),
            pltpu.SemaphoreType.DMA((3,)),
        ],
        compiler_params=params(points, *blocks),
        cost_estimate=COST,
        name="pack",
    )(in_hbm(cluster), in_hbm(points), in_hbm(subcentroids[0]))

    def across(block, g):
        if per == 1:
            return hop("own", owners, g)(block) if g else block
        done = []
        for j in range(per):
            step = g * per + j
            piece = block[j * depth : (j + 1) * depth]
            done.append(hop("own", owners, step)(piece) if step else piece)
        if block.shape[0] > height:
            done.append(block[height:])
        return joined(done)

    def over_chips(block):
        return [block] + [hop("hlp", helpers, step)(block) for step in range(2, helpers, 2)]

    def over_cores(held):
        return [x for block in held for x in (block, hop("hlp", helpers, 1)(block))]

    state = jax.ShapeDtypeStruct((subs + 8, width + 128), F32)
    centre_table = jax.ShapeDtypeStruct((subs, width), BF)

    def scratch(n):
        return [
            state,
            centre_table,
            jax.ShapeDtypeStruct((n * height, subs), BF),
            jax.ShapeDtypeStruct((n * height, width), BF),
        ]

    def semaphores(*counts):
        return [pltpu.SemaphoreType.DMA((n,)) for n in counts]

    beside = hop("hlp", helpers, 1)
    moved = [across(packed[0], 0)]
    for g in range(1, groups - 1):
        moved.append(across(packed[g], g))
    moved.append(across(after(packed[-1], moved[-1]) if groups > 1 else packed[-1], groups - 1))
    held = [over_chips(block) for block in moved]
    own_beside = beside(after(moved[0], held[0][1]))
    rows = [[moved[0], own_beside] + over_cores(held[0][1:])] + [over_cores(part) for part in held[1:-1]]
    given = [r for part in rows for r in part] + over_cores(held[-1][:1])
    own = scratch(len(given))
    sofar = pl.pallas_call(
        functools.partial(some_kernel, helpers, height),
        out_shape=state,
        in_specs=[HBM] * len(given),
        out_specs=HBM,
        scratch_shapes=[pltpu.VMEM(s.shape, s.dtype) for s in own] + semaphores(len(given), helpers, 1),
        compiler_params=params(*own),
        cost_estimate=COST,
        name="some_rows",
    )(*given)
    late = over_cores(held[-1][1:-1] + [after(held[-1][-1], sofar)])
    earlier = given
    logs = [jax.ShapeDtypeStruct((height, subs), BF)] * groups
    refined = jax.ShapeDtypeStruct((share_rows, width), F32)
    own = scratch(len(earlier) + len(late)) + [state, refined]
    refined, *logs = pl.pallas_call(
        functools.partial(last_kernel, helpers, (len(earlier), len(late), groups), share_rows),
        out_shape=[refined] + logs,
        in_specs=[HBM] * (1 + len(earlier) + len(late)),
        out_specs=[HBM] + vmem(groups),
        scratch_shapes=[pltpu.VMEM(s.shape, s.dtype) for s in own]
        + semaphores(len(earlier) + len(late), helpers, 2),
        compiler_params=params(*own, *logs),
        cost_estimate=COST,
        name="rounds",
    )(sofar, *[in_hbm(r) for r in earlier[: 3 * helpers - 2]], *earlier[3 * helpers - 2 :], *late)

    back = [across(logs[g], g) for g in leaving(groups)]
    places = jax.ShapeDtypeStruct((count, groups * height), BF)
    out = jax.ShapeDtypeStruct((count, subs), F32)
    where = pl.pallas_call(
        functools.partial(places_kernel, depth, owners),
        out_shape=places,
        in_specs=vmem(1),
        out_specs=pl.BlockSpec(memory_space=pltpu.VMEM),
        compiler_params=params(places),
        cost_estimate=COST,
        name="places",
    )(after(cluster, refined))
    log_resp = pl.pallas_call(
        unpack_kernel,
        out_shape=out,
        in_specs=vmem(1 + groups),
        out_specs=pl.BlockSpec(memory_space=pltpu.VMEM),
        compiler_params=params(places, *back, out),
        cost_estimate=COST,
        name="unpack",
    )(where, *back)
    return (refined[None], log_resp)


def solution(mesh):
    in_specs = (
        P(("grp", "own", "hlp"), None),
        P(("grp", "own", "hlp")),
        P(("grp", "own"), "hlp", None),
    )
    out_specs = (P(("grp", "own"), "hlp", None), P(("grp", "own", "hlp"), None))
    return jax.shard_map(
        per_device, mesh=mesh, in_specs=in_specs, out_specs=out_specs, check_vma=False
    )
```
